128 devices in a mesh: row: 16 (over x_hi, y, core), col: 8 (over z, x_lo).
Axes of the slice: x: 4 (x_hi: 2, x_lo: 2; x = x_hi * 2 + x_lo), y: 4, z: 4, core: 2. Of those that a mesh axis runs over, the one named last changes fastest.
Arguments:
- hidden_states: bfloat16 [8192, 5120], P(None, 'row'), may hold values from -30 to 30
- lengths: int32 [32], replicated, may hold values from 64 to 256, as said below
- layer_norm_gain: float32 [5120], replicated, may hold values from 0.5 to 1.5
- layer_norm_bias: float32 [5120], replicated, may hold values from -3 to 3
- weights: float32 [4, 5120, 5120], P(None, ('row', 'col')), may hold values from -0.125 to 0.125
- adapter_down_factors: float32 [4, 64, 5120], replicated, may hold values from -0.1 to 0.1
- adapter_up_factors: float32 [4, 5120, 64], P(None, ('row', 'col')), may hold values from -2 to 2
Outputs:
- mixed: bfloat16 [8192, 5120], P('col', 'row')
The draws below stay inside these ranges and needn't reach their ends.
Inputs may be any that keep to these rules, and one draw needn't show every extreme that they name: `lengths`: every protein has at least 64 residues and at least one has exactly 256.
All inputs are finite; a program needn't handle non-finite values.
Results may differ from the reference program's by a relative error of at most 0.02.
Values may be sent and summed in bfloat16 or wider, within the bound.
A program may use at most 192 MiB of HBM per device.

```python
import jax
import jax.numpy as jnp
from jax import lax

D = 5120
HEADS = 40
HEAD = 128
R = 64
LEN = 256
NPROT = 32
TOKENS = 8192


def draw_lengths(key, part):
    key = jax.random.fold_in(key, 11)
    first_key, second_key = jax.random.split(key)
    drawn = jax.random.randint(first_key, (NPROT,), LEN // 4, LEN + 1)
    longest = jax.random.randint(second_key, (), 0, NPROT)
    return jnp.where(jnp.arange(NPROT) == longest, LEN, drawn).astype(jnp.int32)


def draw_hidden_states(key, part):
    key = jax.random.fold_in(key, 23)
    base_key, row_key, col_key = jax.random.split(key, 3)
    rising = jnp.exp(jnp.log(3.0) * jnp.arange(D, dtype=jnp.float32) / D)[None, :]
    base = jax.random.normal(base_key, (TOKENS, D), jnp.float32)
    row_scale = 10.0 ** jax.random.uniform(row_key, (TOKENS, 1), jnp.float32, 0.0, 1.0)
    col_scale = 10.0 ** jax.random.uniform(col_key, (1, D), jnp.float32, 0.0, 1.0) * rising
    return jnp.clip(0.05 * base * row_scale * col_scale, -30.0, 30.0).astype(jnp.bfloat16)


def draw_adapter_down_factors(key, part):
    key = jax.random.fold_in(key, 31)
    result = jax.random.normal(key, (4, R, D), jnp.float32) * D ** (-0.5)
    return jnp.clip(result, -0.1, 0.1)


def draw_adapter_up_factors(key, part):
    key = jax.random.fold_in(key, 37)
    result = jax.random.normal(key, (4, D, R), jnp.float32) * 0.03
    return jnp.clip(result, -2.0, 2.0)


def block_levels(stream_key, dims, cuts, smallest, largest):
    def one(axis_at, parts):
        draws = jax.random.uniform(jax.random.fold_in(jax.random.fold_in(stream_key, 6), axis_at), (parts,), jnp.float32, smallest / len(cuts), largest / len(cuts))
        return jnp.repeat(jnp.exp(draws), dims[axis_at] // parts).reshape((-1,) + (1,) * (len(dims) - axis_at - 1))

    level = one(*cuts[0])
    for cut in cuts[1:]:
        level = level * one(*cut)
    return level


def centred(stream_key, shape, scale, reach, pieces=(), kind=jnp.bfloat16):
    values = scale * jax.random.normal(stream_key, shape, jnp.float32)
    if pieces:
        values = values * block_levels(stream_key, shape, pieces, -0.22, 0.18)
    return jnp.clip(values, -reach, reach).astype(kind)


def setup_inputs(seed: int = 0) -> dict:
    arg_keys = jax.random.split(jax.random.key(seed), 8)
    hidden_states = draw_hidden_states(jax.random.fold_in(arg_keys[7], 71), 0)
    lengths = draw_lengths(jax.random.fold_in(arg_keys[7], 71), 0)
    layer_norm_gain = jnp.clip(1.0 + 0.1 * jax.random.normal(arg_keys[2], (D,), jnp.float32), 0.5, 1.5)
    layer_norm_bias = centred(arg_keys[3], (D,), 0.5, 3.0, (), jnp.float32)
    weights = centred(arg_keys[4], (4, D, D), (D // 2) ** -0.5, 0.125, ((1, 128),), jnp.float32)
    adapter_down_factors = draw_adapter_down_factors(jax.random.fold_in(arg_keys[7], 71), 0)
    adapter_up_factors = draw_adapter_up_factors(jax.random.fold_in(arg_keys[7], 71), 0)
    return dict(hidden_states=hidden_states, lengths=lengths, layer_norm_gain=layer_norm_gain, layer_norm_bias=layer_norm_bias, weights=weights, adapter_down_factors=adapter_down_factors, adapter_up_factors=adapter_up_factors)


adapter_scale = 2.0
ln_eps = 1e-05

def rotary_tables(length, head_dim):
    half_dim = head_dim // 2
    frequency = 10000.0 ** (-(2.0 * jnp.arange(half_dim, dtype=jnp.float32)) / head_dim)
    angles = jnp.arange(length, dtype=jnp.float32)[:, None] * frequency[None, :]
    angles = jnp.concatenate([angles, angles], axis=1)
    return (jnp.cos(angles), jnp.sin(angles))

def rotate(values, cosine_table, sine_table):
    half_dim = values.shape[-1] // 2
    turned = jnp.concatenate([-values[..., half_dim:], values[..., :half_dim]], axis=-1)
    return values * cosine_table[:, None, :] + turned * sine_table[:, None, :]

def normalize(embedded, first_sum, second_sum, gain_part, bias_part):
    average = first_sum[:, None] / D
    variance = second_sum[:, None] / D - average * average
    return ((embedded - average) * lax.rsqrt(variance + ln_eps) * gain_part + bias_part).astype(jnp.bfloat16)

def reference(hidden_states, lengths, layer_norm_gain, layer_norm_bias, weights, adapter_down_factors, adapter_up_factors):
    merged_weights = (weights + adapter_scale * jnp.einsum('dvc,dcw->dvw', adapter_up_factors, adapter_down_factors, precision=lax.Precision.HIGHEST)).astype(jnp.bfloat16)
    positions = jnp.arange(TOKENS, dtype=jnp.int32)
    is_valid = positions % LEN < lengths[positions // LEN]
    embedded = hidden_states.astype(jnp.float32) * is_valid[:, None].astype(jnp.float32)
    normed = normalize(embedded, lax.optimization_barrier(jnp.sum(embedded, axis=1)), lax.optimization_barrier(jnp.sum(embedded * embedded, axis=1)), layer_norm_gain, layer_norm_bias)
    cosine_table, sine_table = rotary_tables(LEN, HEAD)

    def project(index):
        product = jnp.dot(normed, merged_weights[index].T, preferred_element_type=jnp.float32)
        return product.reshape(NPROT, LEN, HEADS, HEAD)
    queries = rotate(project(0), cosine_table, sine_table).astype(jnp.bfloat16)
    key_rows = rotate(project(1), cosine_table, sine_table).astype(jnp.bfloat16)
    value_rows = project(2).astype(jnp.bfloat16)
    scores = jnp.einsum('pqhd,pkhd->phqk', queries.astype(jnp.float32), key_rows.astype(jnp.float32)) * HEAD ** (-0.5)
    key_valid = jnp.arange(LEN, dtype=jnp.int32)[None, :] < lengths[:, None]
    scores = jnp.where(key_valid[:, None, None, :], scores, -jnp.inf)
    row_max = lax.optimization_barrier(jnp.max(scores, axis=3, keepdims=True))
    exponent = jnp.exp(scores - row_max)
    soft_weights = (exponent / lax.optimization_barrier(jnp.sum(exponent, axis=3, keepdims=True))).astype(jnp.bfloat16)
    attention = jnp.einsum('phqk,pkhd->pqhd', soft_weights.astype(jnp.float32), value_rows.astype(jnp.float32))
    attention = attention.astype(jnp.bfloat16).reshape(TOKENS, D)
    projected = jnp.dot(attention, merged_weights[3].T, preferred_element_type=jnp.float32)
    return (embedded + projected).astype(jnp.bfloat16)
```

```python
import jax
import jax.numpy as jnp
from jax import lax
from jax.sharding import PartitionSpec as P

D = 5120
HEAD = 128
HALF = 64
LEN = 256

adapter_scale = 2.0
ln_eps = 1e-05


def rotary_tables(length, head_dim):
    half_dim = head_dim // 2
    frequency = 10000.0 ** (-(2.0 * jnp.arange(half_dim, dtype=jnp.float32)) / head_dim)
    angles = jnp.arange(length, dtype=jnp.float32)[:, None] * frequency[None, :]
    angles = jnp.concatenate([angles, angles], axis=1)
    return (jnp.cos(angles), jnp.sin(angles))


def rotate(values, cosine_table, sine_table):
    half_dim = values.shape[-1] // 2
    turned = jnp.concatenate([-values[..., half_dim:], values[..., :half_dim]], axis=-1)
    return values * cosine_table[:, None, :] + turned * sine_table[:, None, :]


def contract_last(left_rows, right_rows):
    return lax.dot_general(
        left_rows, right_rows, (((1,), (1,)), ((), ())), preferred_element_type=jnp.float32
    )


def attend(qkv, lengths, cosine_table, sine_table):
    queries = rotate(qkv[0], cosine_table, sine_table).astype(jnp.bfloat16)
    key_rows = rotate(qkv[1], cosine_table, sine_table).astype(jnp.bfloat16)
    value_rows = qkv[2].astype(jnp.bfloat16)
    scores = jnp.einsum(
        "pqhd,pkhd->phqk", queries, key_rows, preferred_element_type=jnp.float32
    ) * HEAD ** (-0.5)
    key_valid = jnp.arange(LEN, dtype=jnp.int32)[None, :] < lengths[:, None]
    scores = jnp.where(key_valid[:, None, None, :], scores, -jnp.inf)
    row_max = jnp.max(scores, axis=3, keepdims=True)
    exponent = jnp.exp(scores - row_max)
    soft = (exponent / jnp.sum(exponent, axis=3, keepdims=True)).astype(jnp.bfloat16)
    out = jnp.einsum("phqk,pkhd->pqhd", soft, value_rows, preferred_element_type=jnp.float32)
    out = out.astype(jnp.bfloat16)
    return out.reshape(out.shape[0] * LEN, -1)


def per_device(
    hidden_states,
    lengths,
    layer_norm_gain,
    layer_norm_bias,
    weights,
    adapter_down_factors,
    adapter_up_factors,
):
    col_count = lax.axis_size("col")
    row_count = lax.axis_size("row")
    row_idx = lax.axis_index("row")
    col_idx = lax.axis_index("col")
    core = row_idx % 2
    tokens = hidden_states.shape[0] // col_count
    proteins = tokens // LEN
    first = col_idx * tokens
    own = lax.dynamic_slice_in_dim(hidden_states, first, tokens, 0)
    states = lax.all_gather(own, "row", axis=1, tiled=True)
    merged = (
        weights
        + adapter_scale
        * jnp.einsum(
            "dvc,dcw->dvw",
            adapter_up_factors,
            adapter_down_factors,
            precision=lax.Precision.HIGHEST,
        )
    ).astype(jnp.bfloat16)
    local_lengths = lax.dynamic_slice_in_dim(lengths, col_idx * proteins, proteins, 0)
    valid = (jnp.arange(LEN, dtype=jnp.int32)[None, :] < local_lengths[:, None]).reshape(tokens)
    mask = valid[:, None].astype(jnp.float32)
    block = lax.all_gather(merged[:3], "col", axis=1, tiled=True)
    out_block = lax.all_gather(merged[3], "col", axis=0, tiled=True)
    part = block.shape[1]

    embedded = states.astype(jnp.float32) * mask
    average = jnp.sum(embedded, axis=1)[:, None] / D
    variance = jnp.sum(embedded * embedded, axis=1)[:, None] / D - average * average
    normed = (
        (embedded - average) * lax.rsqrt(variance + ln_eps) * layer_norm_gain + layer_norm_bias
    ).astype(jnp.bfloat16)
    qkv = contract_last(normed, block.reshape(3 * part, D)).reshape(tokens, 3, part)
    whole = part // HEAD * HEAD
    mine = lax.dynamic_slice_in_dim(qkv, core * HALF, whole, 2)
    half = lax.dynamic_slice_in_dim(qkv, (1 - core) * whole, HALF, 2)
    half_tokens = tokens // 2
    keep = lax.dynamic_slice_in_dim(half, core * half_tokens, half_tokens, 0)
    send = lax.dynamic_slice_in_dim(half, (1 - core) * half_tokens, half_tokens, 0)
    got = lax.ppermute(send, "row", [(i, i ^ 1) for i in range(row_count)])
    split = jnp.where(
        core == 0,
        jnp.concatenate([keep, got], axis=2),
        jnp.concatenate([got, keep], axis=2),
    )
    cosine_table, sine_table = rotary_tables(LEN, HEAD)
    mine = mine.transpose(1, 0, 2).reshape(3, proteins, LEN, whole // HEAD, HEAD)
    split = split.transpose(1, 0, 2).reshape(3, proteins // 2, LEN, 1, HEAD)
    split_lengths = lax.dynamic_slice_in_dim(local_lengths, core * (proteins // 2), proteins // 2, 0)
    attn_a = attend(mine, local_lengths, cosine_table, sine_table)
    attn_b = attend(split, split_lengths, cosine_table, sine_table)
    both = jnp.concatenate([attn_a, attn_b.reshape(tokens, HALF)], axis=1)
    got = lax.all_gather(both, "row", axis=0)
    all_a = got[:, :, :whole].reshape(row_count // 2, 2, tokens, whole)
    all_b = got[:, :, whole:].reshape(row_count // 2, tokens, HEAD)
    heads = jnp.concatenate([all_a[:, 0], all_b, all_a[:, 1]], axis=2)
    heads = heads.transpose(1, 0, 2).reshape(tokens, D)
    projected = contract_last(heads, out_block)
    residual = own.astype(jnp.float32) * mask
    return (residual + projected).astype(jnp.bfloat16)


def solution(mesh):
    in_specs = (
        P(None, "row"),
        P(),
        P(),
        P(),
        P(None, ("row", "col"), None),
        P(),
        P(None, ("row", "col"), None),
    )
    out_specs = P("col", "row")
    return jax.shard_map(
        per_device, mesh=mesh, in_specs=in_specs, out_specs=out_specs, check_vma=False
    )
```

```python
import functools

import jax
import jax.numpy as jnp
from jax import lax
from jax.experimental import pallas as pl
from jax.experimental.pallas import tpu as pltpu
from jax.sharding import PartitionSpec as P

MESH = pl.DeviceIdType.MESH
D = 5120
HEAD = 128
HALF = 64
LEN = 256

adapter_scale = 2.0
ln_eps = 1e-05

def plan(do_t, do_w, t_rows, t_cols, w_rows, w_cols, w_first, t_chunk, w_chunk):
    todo = []

    def add(key, link, size, dep, rank):
        todo.append(dict(key=key, link=link, size=size, dep=dep, rank=rank))

    if do_t:
        n = t_rows // t_chunk
        size = t_chunk * t_cols * 2
        for ch in range(n):
            first, second = ("xl", "cross") if ch < n // 2 else ("cross", "xl")
            add(("t", "hop", 0, 0, ch), first, size, None, 0)
            add(("t", "far", 0, 0, ch), second, size, ("t", "hop", 0, 0, ch), 0)
            for other in (0, 1):
                dep = None if other == 0 else ("t", "far", 0, 0, ch)
                for step in (1, -1):
                    add(("t", "ring", step, other, ch), ("y", step), size, dep, other)
                step = 1 if ch < n // 2 else -1
                add(("t", "pass", step, other, ch), ("y", step), size, ("t", "ring", step, other, ch), 2 + other)
                add(("t", "pair", 0, other, ch), "core", size, dep, 0)
                for step in (1, -1):
                    add(("t", "pair", step, other, ch), "core", size, ("t", "ring", step, other, ch), 0)
                step = 1 if ch < n // 2 else -1
                add(("t", "pair", 2, other, ch), "core", size, ("t", "pass", step, other, ch), 0)
    if do_w:
        n = w_rows // w_chunk
        for ch in range(n):
            step2 = 1 if ch < n // 2 else -1
            size = w_chunk * w_first * 2
            if w_first:
                for step in (1, -1):
                    add(("p", "ring", step, 0, ch), ("z", step), size, None, 1)
                    add(("p", "x", step, 0, ch), "xl", size, ("p", "ring", step, 0, ch), 1)
                add(("p", "pass", step2, 0, ch), ("z", step2), size, ("p", "ring", step2, 0, ch), 2)
                add(("p", "x", 0, 0, ch), "xl", size, None, 1)
                add(("p", "x", 2, 0, ch), "xl", size, ("p", "pass", step2, 0, ch), 2)
            size = w_chunk * (w_cols - w_first) * 2
            add(("s", "x", 0, 0, ch), "xl", size, None, 0)
            for other in (0, 1):
                dep = None if other == 0 else ("s", "x", 0, 0, ch)
                for step in (1, -1):
                    add(("s", "ring", step, other, ch), ("z", step), size, dep, other)
                add(("s", "pass", step2, other, ch), ("z", step2), size, ("s", "ring", step2, other, ch), 2 + other)

    arrive = {None: 0.0}
    free = {}
    events = []
    left = list(todo)
    while left:
        best = None
        for t in left:
            if t["dep"] in arrive:
                start = max(arrive[t["dep"]] + 1.0, free.get(t["link"], 0.0))
                score = (start, t["rank"])
                if best is None or score < best[0]:
                    best = (score, t, start)
        _, t, start = best
        rate = 300e3 if t["link"] == "core" else 50e3
        end = start + t["size"] / rate
        free[t["link"]] = end
        arrive[t["key"]] = end
        events.append((start, t))
        left.remove(t)
    return events, arrive


def gather_kernel(cfg, *refs):
    do_t, do_w = cfg["do_t"], cfg["do_w"]
    refs = list(refs)
    t_ref = refs.pop(0) if do_t else None
    w_ref = refs.pop(0) if do_w else None
    t_all = refs.pop(0) if do_t else None
    w_all = refs.pop(0) if do_w else None
    send, recv, local = refs[:3]
    relay = refs[3] if do_t else None
    row, col = lax.axis_index("row"), lax.axis_index("col")
    xh, y, core = row // 8, row // 2 % 4, row % 2
    z, xl = col // 2, col % 2

    def at(dxh=0, dy=0, dcore=0, dz=0, dxl=0):
        r = (xh + dxh) % 2 * 8 + (y + dy + 4) % 4 * 2 + (core + dcore) % 2
        c = (z + dz + 4) % 4 * 2 + (xl + dxl) % 2
        return r, c

    events, arrive = plan(**cfg)
    t_chunk, w_chunk, w_first = cfg["t_chunk"], cfg["w_chunk"], cfg["w_first"]
    peers = []
    if do_t:
        peers += [at(dxh=1, dxl=1), at(dy=1), at(dy=-1), at(dcore=1)]
    if do_w:
        peers += [at(dz=1), at(dz=-1)]
    peers += [at(dxl=1)]
    barrier = pltpu.get_barrier_semaphore()
    for peer in peers:
        pl.semaphore_signal(barrier, inc=1, device_id=peer, device_id_type=MESH)
    own = []
    if do_t:
        own.append(pltpu.make_async_copy(t_ref, t_all.at[row], local.at[0]))
    if do_w:
        own.append(pltpu.make_async_copy(w_ref, w_all.at[col], local.at[1]))
    for c in own:
        c.start()
    pl.semaphore_wait(barrier, len(peers))

    copies = {}
    waited = set()

    def make(i, t):
        kind, what, step, other, ch = t["key"]
        if kind == "t":
            rows = pl.ds(ch * t_chunk, t_chunk)
            one, two = at(dxl=1), at(dxh=1, dxl=1)
            if ch >= cfg["t_rows"] // t_chunk // 2:
                one, two = two, one
            if what == "hop":
                return pltpu.make_async_remote_copy(
                    src_ref=t_ref.at[rows], dst_ref=relay.at[rows], send_sem=send.at[i],
                    recv_sem=recv.at[i], device_id=one, device_id_type=MESH,
                )
            if what == "far":
                slot = at() if ch < cfg["t_rows"] // t_chunk // 2 else at(dxh=1)
                return pltpu.make_async_remote_copy(
                    src_ref=relay.at[rows], dst_ref=t_all.at[slot[0], rows], send_sem=send.at[i],
                    recv_sem=recv.at[i], device_id=two, device_id_type=MESH,
                )
            elif what == "ring":
                slot, to = at(dxh=other), at(dy=step)
            elif what == "pass":
                slot, to = at(dxh=other, dy=-step), at(dy=step)
            else:
                slot, to = at(dxh=other, dy=-step), at(dcore=1)
            mine = what == "ring" and other == 0 or what == "pair" and step == 0 and other == 0
            dst = t_all.at[slot[0], rows]
            src = t_ref.at[rows] if mine else dst
        else:
            rows = pl.ds(ch * w_chunk, w_chunk)
            cols = pl.ds(0, w_first) if kind == "p" else pl.ds(w_first, cfg["w_cols"] - w_first)
            if what == "x":
                slot, to = at(dz=-step), at(dxl=1)
            elif what == "ring":
                slot, to = at(dxl=other), at(dz=step)
            else:
                slot, to = at(dxl=other, dz=-step), at(dz=step)
            mine = other == 0 and (what == "ring" or what == "x" and step == 0)
            dst = w_all.at[slot[1], rows, cols]
            src = w_ref.at[rows, cols] if mine else dst
        return pltpu.make_async_remote_copy(
            src_ref=src, dst_ref=dst, send_sem=send.at[i], recv_sem=recv.at[i],
            device_id=to, device_id_type=MESH,
        )

    for i, (_, t) in enumerate(events):
        dep = t["dep"]
        if dep is not None and dep not in waited:
            copies[dep].wait_recv()
            waited.add(dep)
        copies[t["key"]] = make(i, t)
        copies[t["key"]].start()
    for key in sorted(copies, key=lambda k: arrive[k]):
        if key not in waited:
            copies[key].wait_recv()
    for key in copies:
        copies[key].wait_send()
    for c in own:
        c.wait()


def gather(t, w, w_first, t_chunk=80, w_chunk=32, collective_id=0):
    do_t, do_w = t is not None, w is not None
    cfg = dict(
        do_t=do_t, do_w=do_w,
        t_rows=t.shape[0] if do_t else 0, t_cols=t.shape[1] if do_t else 0,
        w_rows=w.shape[0] if do_w else 0, w_cols=w.shape[1] if do_w else 0,
        w_first=w_first, t_chunk=t_chunk, w_chunk=w_chunk,
    )
    count = len(plan(**cfg)[0])
    out = []
    if do_t:
        out.append(jax.ShapeDtypeStruct((16,) + t.shape, t.dtype))
    if do_w:
        out.append(jax.ShapeDtypeStruct((8,) + w.shape, w.dtype))
    args = [a for a in (t, w) if a is not None]
    return pl.pallas_call(
        functools.partial(gather_kernel, cfg),
        out_shape=out,
        in_specs=[pl.BlockSpec(memory_space=pl.ANY)] * len(args),
        out_specs=[pl.BlockSpec(memory_space=pl.ANY)] * len(args),
        scratch_shapes=[
            pltpu.SemaphoreType.DMA((count,)),
            pltpu.SemaphoreType.DMA((count,)),
            pltpu.SemaphoreType.DMA((2,)),
        ] + ([pltpu.VMEM(t.shape, t.dtype)] if do_t else []),
        compiler_params=pltpu.CompilerParams(collective_id=collective_id, has_side_effects=True),
    )(*args)


def rotary_tables(length, head_dim):
    half_dim = head_dim // 2
    frequency = 10000.0 ** (-(2.0 * jnp.arange(half_dim, dtype=jnp.float32)) / head_dim)
    angles = jnp.arange(length, dtype=jnp.float32)[:, None] * frequency[None, :]
    angles = jnp.concatenate([angles, angles], axis=1)
    return (jnp.cos(angles), jnp.sin(angles))


def attend(qkv, lengths, cosine, sine):
    def rotate(u):
        turned = jnp.concatenate([-u[:, HALF:], u[:, :HALF]], axis=1)
        return (u * cosine[None, :, None] + turned * sine[None, :, None]).astype(jnp.bfloat16)

    queries, key_rows, value_rows = rotate(qkv[0]), rotate(qkv[1]), qkv[2].astype(jnp.bfloat16)
    scores = jnp.einsum(
        "hdpq,hdpk->hpkq", queries, key_rows, preferred_element_type=jnp.float32
    ) * HEAD ** (-0.5)
    key_valid = jnp.arange(LEN, dtype=jnp.int32)[None, :] < lengths[:, None]
    scores = jnp.where(key_valid[None, :, :, None], scores, -jnp.inf)
    exponent = jnp.exp(scores - jnp.max(scores, axis=2, keepdims=True))
    soft = (exponent / jnp.sum(exponent, axis=2, keepdims=True)).astype(jnp.bfloat16)
    out = jnp.einsum("hpkq,hdpk->hdpq", soft, value_rows, preferred_element_type=jnp.float32)
    return out.astype(jnp.bfloat16).reshape(out.shape[0] * HEAD, -1)


def per_device(
    hidden_states,
    lengths,
    layer_norm_gain,
    layer_norm_bias,
    weights,
    adapter_down_factors,
    adapter_up_factors,
):
    col_count = lax.axis_size("col")
    row_count = lax.axis_size("row")
    row_idx = lax.axis_index("row")
    col_idx = lax.axis_index("col")
    core = row_idx % 2
    tokens = hidden_states.shape[0] // col_count
    proteins = tokens // LEN
    own = lax.dynamic_slice_in_dim(hidden_states, col_idx * tokens, tokens, 0)
    merged = (
        weights
        + adapter_scale
        * jnp.einsum(
            "dvc,dcw->dvw",
            adapter_up_factors,
            adapter_down_factors,
            precision=lax.Precision.HIGHEST,
        )
    ).astype(jnp.bfloat16)
    shard = merged.shape[1]
    merged = merged.reshape(4 * shard, D)
    states, block = gather(own.T, merged[:128], 1664, 160, 64, collective_id=0)
    local_lengths = lax.dynamic_slice_in_dim(lengths, col_idx * proteins, proteins, 0)
    valid = (jnp.arange(LEN, dtype=jnp.int32)[None, :] < local_lengths[:, None]).reshape(tokens)
    mask = valid[None, :].astype(jnp.float32)

    embedded = states.reshape(D, tokens).astype(jnp.float32) * mask
    average = jnp.sum(embedded, axis=0)[None, :] / D
    variance = jnp.sum(embedded * embedded, axis=0)[None, :] / D - average * average
    normed = (
        (embedded - average) * lax.rsqrt(variance + ln_eps) * layer_norm_gain[:, None]
        + layer_norm_bias[:, None]
    ).astype(jnp.bfloat16)
    out = jnp.dot(block.reshape(col_count * 128, D), normed, preferred_element_type=jnp.float32)
    out = out.reshape(col_count, 128, tokens)
    part = col_count * shard
    qkv = out[:, : 3 * shard].reshape(col_count, 3, shard, tokens)
    qkv = qkv.transpose(1, 0, 2, 3).reshape(3, part, tokens)
    whole = part // HEAD * HEAD
    mine = lax.dynamic_slice_in_dim(qkv, core * HALF, whole, 1)
    half = lax.dynamic_slice_in_dim(qkv, (1 - core) * whole, HALF, 1)
    half_tokens = tokens // 2
    keep = lax.dynamic_slice_in_dim(half, core * half_tokens, half_tokens, 2)
    send = lax.dynamic_slice_in_dim(half, (1 - core) * half_tokens, half_tokens, 2)
    got = lax.ppermute(send, "row", [(i, i ^ 1) for i in range(row_count)])
    split = jnp.where(
        core == 0,
        jnp.concatenate([keep, got], axis=1),
        jnp.concatenate([got, keep], axis=1),
    )
    cosine, sine = rotary_tables(LEN, HEAD)
    cosine, sine = cosine.T, sine.T
    mine = mine.reshape(3, whole // HEAD, HEAD, proteins, LEN)
    split = split.reshape(3, 1, HEAD, proteins // 2, LEN)
    split_lengths = lax.dynamic_slice_in_dim(local_lengths, core * (proteins // 2), proteins // 2, 0)
    attn_a = attend(mine, local_lengths, cosine, sine)
    attn_b = attend(split, split_lengths, cosine, sine)
    attn_b = jnp.concatenate([attn_b[:HALF], attn_b[HALF:]], axis=1)
    both = jnp.concatenate([attn_a, attn_b], axis=0)
    got, rest = gather(both, merged[128:], 1664, 160, 16, collective_id=1)
    all_a = got[:, :whole].reshape(row_count // 2, 2, whole, tokens)
    all_b = got[:, whole:].reshape(row_count // 2, 2, HALF, 2, half_tokens)
    all_b = all_b.transpose(0, 3, 2, 1, 4).reshape(row_count // 2, HEAD, tokens)
    heads = jnp.concatenate([all_a[:, 0], all_b, all_a[:, 1]], axis=1).reshape(D, tokens)
    out_block = jnp.concatenate([block[:, 3 * shard :], rest], axis=1).reshape(part, D)
    projected = jnp.dot(out_block, heads, preferred_element_type=jnp.float32).T
    residual = own.astype(jnp.float32) * mask[0][:, None]
    return (residual + projected).astype(jnp.bfloat16)


def solution(mesh):
    in_specs = (
        P(None, "row"),
        P(),
        P(),
        P(),
        P(None, ("row", "col"), None),
        P(),
        P(None, ("row", "col"), None),
    )
    out_specs = P("col", "row")
    return jax.shard_map(
        per_device, mesh=mesh, in_specs=in_specs, out_specs=out_specs, check_vma=False
    )
```

```python
import functools

import jax
import jax.numpy as jnp
from jax import lax
from jax.experimental import pallas as pl
from jax.experimental.pallas import tpu as pltpu
from jax.sharding import PartitionSpec as P

MESH = pl.DeviceIdType.MESH
D = 5120
HEAD = 128
HALF = 64
LEN = 256
TOK = 1024
PART = 320
SHARD = 40
W1 = 128
W2 = 48
W2_FROM = 112
FIRST = 1664

adapter_scale = 2.0
ln_eps = 1e-05

T1_CHUNKS = [(0, 160), (160, 320)]
COLS = {"p": [(0, 768), (768, FIRST)], "s": [(FIRST, 3456), (3456, D)]}


def transfers():
    todo = []

    def add(key, link, size, deps, rank):
        todo.append(dict(key=key, link=link, size=size, deps=deps, rank=rank, time=None))

    def slots(kind, sizes, ready, rank):
        n = len(sizes)
        for ch, size in enumerate(sizes):
            up = ch < n // 2 if kind == "a" else ch % 2 == 0
            step2 = 1 if up else -1
            first, second = ("xl", "cross") if up else ("cross", "xl")
            start = ready(ch)
            add((kind, "hop", 0, 0, ch), first, size, start, rank)
            add((kind, "far", 0, 0, ch), second, size, [(kind, "hop", 0, 0, ch)], rank)
            for other in (0, 1):
                deps = start if other == 0 else [(kind, "far", 0, 0, ch)]
                for step in (1, -1):
                    add((kind, "ring", step, other, ch), ("y", step), size, deps, rank + other)
                ring = (kind, "ring", step2, other, ch)
                add((kind, "pass", step2, other, ch), ("y", step2), size, [ring], rank + 2 + other)
                add((kind, "pair", 0, other, ch), "core", size, deps, rank)
                for step in (1, -1):
                    add((kind, "pair", step, other, ch), "core", size, [(kind, "ring", step, other, ch)], rank)
                add((kind, "pair", 2, other, ch), "core", size, [(kind, "pass", step2, other, ch)], rank)

    def rows(kind, count, rank):
        for ch in (0, 1):
            step2 = 1 if ch == 0 else -1
            p, s = kind + "p", kind + "s"
            size = count * (COLS["p"][ch][1] - COLS["p"][ch][0]) * 2
            for step in (1, -1):
                add((p, "ring", step, 0, ch), ("z", step), size, [], rank + 1)
                add((p, "x", step, 0, ch), "xl", size, [(p, "ring", step, 0, ch)], rank + 1)
            add((p, "pass", step2, 0, ch), ("z", step2), size, [(p, "ring", step2, 0, ch)], rank + 2)
            add((p, "x", 0, 0, ch), "xl", size, [], rank + 1)
            add((p, "x", 2, 0, ch), "xl", size, [(p, "pass", step2, 0, ch)], rank + 2)
            size = count * (COLS["s"][ch][1] - COLS["s"][ch][0]) * 2
            add((s, "x", 0, 0, ch), "xl", size, [], rank)
            for other in (0, 1):
                deps = [] if other == 0 else [(s, "x", 0, 0, ch)]
                for step in (1, -1):
                    add((s, "ring", step, other, ch), ("z", step), size, deps, rank + other)
                ring = (s, "ring", step2, other, ch)
                add((s, "pass", step2, other, ch), ("z", step2), size, [ring], rank + 2 + other)

    slots("a", [(b - a) * TOK * 2 for a, b in T1_CHUNKS], lambda ch: [], 0)
    rows("v", W1, 1)
    rows("o", W2, 20)
    slots("b", [r * LEN * 2 for r in (256, 256, 384, 384)], lambda ch: [("attend", ch)], 10)
    for step in (0, 1):
        add(("h", "half", 0, 0, step), "core", 3 * HALF * LEN * 4, [("qkv", step)], -1)
    return todo


def step2_of(kind, ch):
    up = ch == 0 if kind == "a" else ch % 2 == 0
    return 1 if up else -1


def arrival(kind, step, other, ch):
    if step == 0:
        return [(kind, "far", 0, 0, ch)] if other else []
    if step == 2:
        return [(kind, "pass", step2_of(kind, ch), other, ch)]
    return [(kind, "ring", step, other, ch)]


def weight_keys(kind):
    return [t["key"] for t in transfers() if t["key"][0] in (kind + "p", kind + "s")]


def computes():
    todo = []

    def add(key, time, deps, rank, sends=()):
        todo.append(dict(key=key, time=time, deps=deps, rank=rank, sends=list(sends), link=None))

    spots = [(other, step) for other in (0, 1) for step in (0, 1, -1, 2)]
    stats = []
    for other, step in spots:
        for twin in (0, 1):
            deps = []
            for ch in range(len(T1_CHUNKS)):
                deps += [("a", "pair", step, other, ch)] if twin else arrival("a", step, other, ch)
            add(("stat", other, step, twin), 0.6, deps, 0)
            stats.append(("stat", other, step, twin))
    add(("moments",), 0.2, stats, 1)
    for other, step in spots:
        for twin in (0, 1):
            sends = []
            if not twin:
                for ch in range(len(T1_CHUNKS)):
                    if (other, step) != (0, 0):
                        sends.append(("a", "pair", step, other, ch))
                    if step == 0 and other == 1:
                        sends += [("a", "ring", 1, 1, ch), ("a", "ring", -1, 1, ch)]
                    if step == step2_of("a", ch):
                        sends.append(("a", "pass", step, other, ch))
            add(("norm", other, step, twin), 0.8, [("moments",)], 2, sends)
    norms = [("norm", o, s, t) for o, s in spots for t in (0, 1)]
    for s in range(4):
        add(("qkv", s), 3.2, norms + weight_keys("v"), 3 + s)
        deps = [("qkv", s)] + ([("h", "half", 0, 0, s - 2)] if s >= 2 else [])
        add(("attend", s), 1.5 if s < 2 else 2.2, deps, 2.5)
    for other, step in spots:
        for twin in (0, 1):
            for pair in (0, 1):
                deps = weight_keys("o")
                for ch in (2 * pair, 2 * pair + 1):
                    if twin:
                        deps += [("b", "pair", step, other, ch)]
                    elif (other, step) == (0, 0):
                        deps += [("attend", ch)]
                    else:
                        deps += arrival("b", step, other, ch)
                add(("out", other, step, twin, pair), 0.6, deps, 50)
    return todo


def schedule():
    left = transfers() + computes()
    done, free, order, now = {}, {}, [], 0.0
    while left:
        best, later = None, []
        for t in left:
            if not all(d in done for d in t["deps"]):
                continue
            ready = max([0.0] + [done[d] for d in t["deps"]])
            if t["link"] is not None:
                ready = max(ready, free.get(t["link"], 0.0) - 6.0)
            if ready > now:
                later.append(ready)
                continue
            score = (t["link"] is None, t["rank"])
            if best is None or score < best[0]:
                best = (score, t)
        if best is None:
            now = min(later)
            continue
        t = best[1]
        if t["link"] is None:
            now += t["time"]
            done[t["key"]] = now
        else:
            now += 0.1
            rate = 200e3 if t["link"] == "core" else 45e3
            end = max(now, free.get(t["link"], 0.0)) + t["size"] / rate
            free[t["link"]] = end
            done[t["key"]] = end + 1.5
        order.append(t)
        left.remove(t)
    return order, done


def fused(
    t_ref, w_ref, mask_ref, bias_ref, affine_ref, cos_ref, sin_ref, out_ref,
    t1, w1, w2, t2, relay1, relay2, qkv_s, half_s, sums, moments, acc, send, recv, local,
):
    row, col = lax.axis_index("row"), lax.axis_index("col")
    xh, y, core = row // 8, row // 2 % 4, row % 2
    z, xl = col // 2, col % 2

    def at(dxh=0, dy=0, dcore=0, dz=0, dxl=0):
        r = (xh + dxh) % 2 * 8 + (y + dy + 4) % 4 * 2 + (core + dcore) % 2
        c = (z + dz + 4) % 4 * 2 + (xl + dxl) % 2
        return r, c

    order, done = schedule()
    peers = [at(dy=1), at(dy=-1), at(dcore=1), at(dz=1), at(dz=-1), at(dxl=1), at(dxh=1, dxl=1)]
    barrier = pltpu.get_barrier_semaphore()
    for peer in peers:
        pl.semaphore_signal(barrier, inc=1, device_id=peer, device_id_type=MESH)
    own = [
        pltpu.make_async_copy(t_ref, t1.at[pl.ds(row * PART, PART)], local.at[0]),
        pltpu.make_async_copy(w_ref.at[pl.ds(0, W1)], w1.at[pl.ds(col * W1, W1)], local.at[1]),
        pltpu.make_async_copy(w_ref.at[pl.ds(W2_FROM, W2)], w2.at[pl.ds(col * W2, W2)], local.at[2]),
    ]
    for c in own:
        c.start()
    sums[...] = jnp.zeros_like(sums)
    acc[...] = jnp.zeros_like(acc)
    pl.semaphore_wait(barrier, len(peers))

    def protein(c, s):
        return (2 * (1 - c) + s) % 4

    def make(i, key):
        kind, what, step, other, ch = key

        def copy(src, dst, to):
            return pltpu.make_async_remote_copy(
                src_ref=src, dst_ref=dst, send_sem=send.at[i], recv_sem=recv.at[i],
                device_id=to, device_id_type=MESH,
            )

        if kind == "h":
            src = qkv_s.at[ch, :, pl.ds((1 - core) * 256, HALF), :]
            return copy(src, half_s.at[ch], at(dcore=1))
        if kind in ("a", "b"):
            def block(r):
                if kind == "a":
                    lo, hi = T1_CHUNKS[ch]
                    return t1.at[pl.ds(r * PART + lo, hi - lo)]
                return t2.at[r, ch, pl.ds(0, 256 if ch < 2 else 384)]

            def via():
                if kind == "a":
                    lo, hi = T1_CHUNKS[ch]
                    return relay1.at[pl.ds(lo, hi - lo)]
                return relay2.at[ch, pl.ds(0, 256 if ch < 2 else 384)]

            def source():
                if kind == "a":
                    lo, hi = T1_CHUNKS[ch]
                    return t_ref.at[pl.ds(lo, hi - lo)]
                return block(row)

            up = step2_of(kind, ch) == 1
            one, two = at(dxl=1), at(dxh=1, dxl=1)
            if not up:
                one, two = two, one
            if what == "hop":
                return copy(source(), via(), one)
            if what == "far":
                return copy(via(), block((at() if up else at(dxh=1))[0]), two)
            if what == "ring":
                slot, to = at(dxh=other), at(dy=step)
            elif what == "pass":
                slot, to = at(dxh=other, dy=-step), at(dy=step)
            else:
                slot, to = at(dxh=other, dy=-step), at(dcore=1)
            mine = other == 0 and (what == "ring" or what == "pair" and step == 0)
            return copy(source() if mine else block(slot[0]), block(slot[0]), to)
        lo, hi = COLS[kind[1]][ch]
        whole, count, first = (w1, W1, 0) if kind[0] == "v" else (w2, W2, W2_FROM)
        if what == "x":
            slot, to = at(dz=-step), at(dxl=1)
        elif what == "ring":
            slot, to = at(dxl=other), at(dz=step)
        else:
            slot, to = at(dxl=other, dz=-step), at(dz=step)
        mine = other == 0 and (what == "ring" or what == "x" and step == 0)
        dst = whole.at[pl.ds(slot[1] * count, count), pl.ds(lo, hi - lo)]
        src = w_ref.at[pl.ds(first, count), pl.ds(lo, hi - lo)] if mine else dst
        return copy(src, dst, to)

    def slot_of(other, step, twin):
        return at(dxh=other, dy=-step, dcore=twin)[0]

    def stat(other, step, twin):
        base = slot_of(other, step, twin) * PART

        def body(i, carry):
            one, two = carry
            x = t1[pl.ds(pl.multiple_of(base + i * 16, 16), 16), :].astype(jnp.float32) * mask_ref[...]
            return one + x[:8] + x[8:], two + x[:8] * x[:8] + x[8:] * x[8:]

        one, two = lax.fori_loop(0, PART // 16, body, (sums[0], sums[1]))
        sums[0] = one
        sums[1] = two

    def get_moments():
        average = jnp.sum(sums[0], axis=0, keepdims=True) / D
        variance = jnp.sum(sums[1], axis=0, keepdims=True) / D - average * average
        moments[0] = average
        moments[1] = lax.rsqrt(variance + ln_eps)

    def norm(other, step, twin):
        base = slot_of(other, step, twin) * PART

        def body(i, carry):
            here = pl.ds(pl.multiple_of(base + i * 16, 16), 16)
            x = t1[here, :].astype(jnp.float32) * mask_ref[...]
            gain = affine_ref[here, 0:1]
            shift = affine_ref[here, 1:2]
            t1[here, :] = ((x - moments[0]) * moments[1] * gain + shift).astype(jnp.bfloat16)
            return carry

        lax.fori_loop(0, PART // 16, body, 0)

    def qkv(s):
        lanes = pl.ds(pl.multiple_of(protein(core, s) * LEN, LEN), LEN)
        for m in range(2):
            result = jnp.dot(
                w1[pl.ds(m * 512, 512), :], t1[:, lanes], preferred_element_type=jnp.float32
            )
            for j in range(4):
                for k in range(3):
                    qkv_s[s, k, pl.ds((m * 4 + j) * SHARD, SHARD), :] = result[
                        j * W1 + k * SHARD : j * W1 + (k + 1) * SHARD
                    ]

    def head(first, second, keys, s, rows):
        cosine, sine = cos_ref[...], sin_ref[...]

        def rotate(k):
            u, v = first[k], second[k]
            return jnp.concatenate([u * cosine - v * sine, v * cosine + u * sine], axis=0).astype(jnp.bfloat16)

        queries, key_rows = rotate(0), rotate(1)
        value_rows = jnp.concatenate([first[2], second[2]], axis=0).astype(jnp.bfloat16)
        scores = lax.dot_general(
            key_rows, queries, (((0,), (0,)), ((), ())), preferred_element_type=jnp.float32
        ) * HEAD ** (-0.5)
        scores = scores + keys
        exponent = jnp.exp(scores - jnp.max(scores, axis=0, keepdims=True))
        soft = (exponent * (1.0 / jnp.sum(exponent, axis=0, keepdims=True))).astype(jnp.bfloat16)
        got = jnp.dot(value_rows, soft, preferred_element_type=jnp.float32)
        t2[row, s, pl.ds(rows, HEAD), :] = got.astype(jnp.bfloat16)

    def attend(s):
        keys = bias_ref[pl.ds(pl.multiple_of(protein(core, s) * LEN, LEN), LEN), :]
        for h in range(2):
            start = core * HALF + h * HEAD
            first = [qkv_s[s, k, pl.ds(pl.multiple_of(start, HALF), HALF), :] for k in range(3)]
            second = [qkv_s[s, k, pl.ds(pl.multiple_of(start + HALF, HALF), HALF), :] for k in range(3)]
            head(first, second, keys, s, h * HEAD)
        if s >= 2:
            first, second = [], []
            for k in range(3):
                mine = qkv_s[s, k, pl.ds(pl.multiple_of((1 - core) * 256, HALF), HALF), :]
                came = half_s[s - 2, k]
                first.append(jnp.where(core == 0, mine, came))
                second.append(jnp.where(core == 0, came, mine))
            head(first, second, keys, s, 256)

    def project(other, step, twin, pair):
        r = slot_of(other, step, twin)
        chip, c = r // 2, r % 2
        cols = pl.ds(pl.multiple_of(chip * 640 + c * 384, 128), 256)
        middle = pl.ds(pl.multiple_of(chip * 640 + 256, 128), 128)
        for s in (2 * pair, 2 * pair + 1):
            p = protein(c, s)
            value = jnp.dot(w2[:, cols], t2[r, s, 0:256, :], preferred_element_type=jnp.float32)
            if pair:
                value += jnp.dot(w2[:, middle], t2[r, s, 256:384, :], preferred_element_type=jnp.float32)
            acc[p] += value

    copies, waited, gone = {}, set(), set()
    local_done = [False]
    for i, t in enumerate(order):
        key = t["key"]
        for dep in t["deps"]:
            if dep in copies and dep not in waited:
                copies[dep].wait_recv()
                waited.add(dep)
        if t["link"] is not None:
            copies[key] = make(len(copies), key)
            copies[key].start()
            continue
        if not local_done[0]:
            for c in own:
                c.wait()
            local_done[0] = True
        for dep in t["sends"]:
            copies[dep].wait_send()
            gone.add(dep)
        dict(stat=stat, moments=get_moments, norm=norm, qkv=qkv, attend=attend, out=project)[key[0]](*key[1:])
    for key in sorted(copies, key=lambda k: done[k]):
        if key not in waited:
            copies[key].wait_recv()
        if key not in gone:
            copies[key].wait_send()
    for j in range(4):
        for p in range(4):
            value = jnp.concatenate(
                [acc[p, pl.ds(96 * j + 8, SHARD), :], acc[p, pl.ds(96 * j + 56, SHARD), :]], axis=0
            )
            lanes = pl.ds(p * LEN, LEN)
            rest = t_ref[pl.ds(80 * j, 80), lanes].astype(jnp.float32) * mask_ref[:, lanes]
            out_ref[pl.ds(80 * j, 80), lanes] = (rest + value).astype(jnp.bfloat16)


def run_fused(states, merged, mask, bias, affine, cosine, sine):
    count = len(transfers())
    vmem = pl.BlockSpec(memory_space=pltpu.VMEM)
    return pl.pallas_call(
        fused,
        out_shape=jax.ShapeDtypeStruct((PART, TOK), jnp.bfloat16),
        in_specs=[vmem] * 7,
        out_specs=vmem,
        scratch_shapes=[
            pltpu.VMEM((D, TOK), jnp.bfloat16),
            pltpu.VMEM((8 * W1, D), jnp.bfloat16),
            pltpu.VMEM((8 * W2, D), jnp.bfloat16),
            pltpu.VMEM((16, 4, 384, LEN), jnp.bfloat16),
            pltpu.VMEM((PART, TOK), jnp.bfloat16),
            pltpu.VMEM((4, 384, LEN), jnp.bfloat16),
            pltpu.VMEM((4, 3, PART, LEN), jnp.float32),
            pltpu.VMEM((2, 3, HALF, LEN), jnp.float32),
            pltpu.VMEM((2, 8, TOK), jnp.float32),
            pltpu.VMEM((2, 1, TOK), jnp.float32),
            pltpu.VMEM((4, 8 * W2, LEN), jnp.float32),
            pltpu.SemaphoreType.DMA((count,)),
            pltpu.SemaphoreType.DMA((count,)),
            pltpu.SemaphoreType.DMA((3,)),
        ],
        compiler_params=pltpu.CompilerParams(
            collective_id=0, has_side_effects=True, vmem_limit_bytes=60 * 1024 * 1024
        ),
    )(states, merged, mask, bias, affine, cosine, sine)


def rotary_tables():
    half_dim = HEAD // 2
    frequency = 10000.0 ** (-(2.0 * jnp.arange(half_dim, dtype=jnp.float32)) / HEAD)
    angles = frequency[:, None] * jnp.arange(LEN, dtype=jnp.float32)[None, :]
    return jnp.cos(angles), jnp.sin(angles)


def per_device(
    hidden_states,
    lengths,
    layer_norm_gain,
    layer_norm_bias,
    weights,
    adapter_down_factors,
    adapter_up_factors,
):
    col_idx = lax.axis_index("col")
    own = lax.dynamic_slice_in_dim(hidden_states, col_idx * TOK, TOK, 0)
    merged = (
        weights
        + adapter_scale
        * jnp.einsum(
            "dvc,dcw->dvw",
            adapter_up_factors,
            adapter_down_factors,
            precision=lax.Precision.HIGHEST,
        )
    ).astype(jnp.bfloat16)
    merged = merged.reshape(4 * SHARD, D)
    proteins = TOK // LEN
    local_lengths = lax.dynamic_slice_in_dim(lengths, col_idx * proteins, proteins, 0)
    valid = (jnp.arange(LEN, dtype=jnp.int32)[None, :] < local_lengths[:, None]).reshape(TOK)
    mask = valid[None, :].astype(jnp.float32)
    bias = jnp.where(valid, 0.0, -jnp.inf).astype(jnp.float32)[:, None]
    affine = jnp.stack([layer_norm_gain, layer_norm_bias], axis=1)
    cosine, sine = rotary_tables()
    return run_fused(own.T, merged, mask, bias, affine, cosine, sine).T


def solution(mesh):
    in_specs = (
        P(None, "row"),
        P(),
        P(),
        P(),
        P(None, ("row", "col"), None),
        P(),
        P(None, ("row", "col"), None),
    )
    out_specs = P("col", "row")
    return jax.shard_map(
        per_device, mesh=mesh, in_specs=in_specs, out_specs=out_specs, check_vma=False
    )
```

```python
import functools

import jax
import jax.numpy as jnp
import numpy as np
from jax import lax
from jax.experimental import pallas as pl
from jax.experimental.pallas import tpu as pltpu
from jax.sharding import PartitionSpec as P

VMEM_BYTES = 60 * 1024 * 1024
MESH = pl.DeviceIdType.MESH
D = 5120
HEAD = 128
HALF = 64
LEN = 256
TOK = 1024
PART = 320
SHARD = 40
W1 = 128
W2 = 48
W2_FROM = 112

adapter_scale = 2.0
ln_eps = 1e-05

T1_CHUNKS = [(0, 160), (160, 320)]


COLS = {"p": [(0, 768), (768, 1792)], "s": [(1792, 3584), (3584, D)]}
LATE = (3,)
SLACK = 3.0


def transfers():
    todo = []

    def add(key, link, size, deps, rank):
        todo.append(dict(key=key, link=link, size=size, deps=deps, rank=rank, time=None))

    def slots(kind, sizes, ready, rank):
        n = len(sizes)
        for ch, size in enumerate(sizes):
            up = ch < n // 2 if kind == "a" else ch % 2 == 0
            step2 = 1 if up else -1
            first, second = ("xl", "cross") if up else ("cross", "xl")
            start = ready(ch)
            late = kind == "b" and ch in LATE
            add((kind, "hop", 0, 0, ch), first, size, start, rank)
            add((kind, "far", 0, 0, ch), second, size, [(kind, "hop", 0, 0, ch)], rank)
            for other in (0, 1):
                deps = start if other == 0 else [(kind, "far", 0, 0, ch)]
                if late and other:
                    add((kind, "pair", 0, 1, ch), "core", size, deps, rank)
                    for step in (1, -1, 2):
                        first, second = second, first
                        came = (kind, "pass" if step == 2 else "ring", step2 if step == 2 else step, 0, ch)
                        add((kind, "hop", step, 0, ch), first, size, [came], rank + 1)
                        add((kind, "far", step, 0, ch), second, size, [(kind, "hop", step, 0, ch)], rank + 1)
                        add((kind, "pair", step, 1, ch), "core", size, [(kind, "far", step, 0, ch)], rank)
                    continue
                for step in (1, -1):
                    add((kind, "ring", step, other, ch), ("y", step), size, deps, rank + other)
                ring = (kind, "ring", step2, other, ch)
                add((kind, "pass", step2, other, ch), ("y", step2), size, [ring], rank + 2 + other)
                add((kind, "pair", 0, other, ch), "core", size, deps, rank)
                for step in (1, -1):
                    add((kind, "pair", step, other, ch), "core", size, [(kind, "ring", step, other, ch)], rank)
                add((kind, "pair", 2, other, ch), "core", size, [(kind, "pass", step2, other, ch)], rank)

    def rows(kind, count, rank):
        for ch in (0, 1):
            step2 = 1 if ch == 0 else -1
            p, s = kind + "p", kind + "s"
            own_p, own_s = [("merge", "p", ch)], [("merge", "s", ch)]
            size = count * (COLS["p"][ch][1] - COLS["p"][ch][0]) * 2
            for step in (1, -1):
                add((p, "ring", step, 0, ch), ("z", step), size, own_p, rank + 1)
                add((p, "x", step, 0, ch), "xl", size, [(p, "ring", step, 0, ch)], rank + 1)
            add((p, "pass", step2, 0, ch), ("z", step2), size, [(p, "ring", step2, 0, ch)], rank + 2)
            add((p, "x", 0, 0, ch), "xl", size, own_p, rank + 1)
            add((p, "x", 2, 0, ch), "xl", size, [(p, "pass", step2, 0, ch)], rank + 2)
            size = count * (COLS["s"][ch][1] - COLS["s"][ch][0]) * 2
            add((s, "x", 0, 0, ch), "xl", size, own_s, rank)
            for other in (0, 1):
                deps = own_s if other == 0 else [(s, "x", 0, 0, ch)]
                for step in (1, -1):
                    add((s, "ring", step, other, ch), ("z", step), size, deps, rank + other)
                ring = (s, "ring", step2, other, ch)
                add((s, "pass", step2, other, ch), ("z", step2), size, [ring], rank + 2 + other)

    slots("a", [(b - a) * TOK * 2 for a, b in T1_CHUNKS], lambda ch: [], 0)
    rows("v", W1, 1)
    rows("o", W2, 20)
    slots("b", [r * LEN * 2 for r in (256, 256, 384, 384)], lambda ch: [("attend", ch)], 10)
    for step in (0, 1):
        add(("h", "half", 0, 0, step), "core", 3 * HALF * LEN * 4, [("qkv", step)], -1)
    return todo


def step2_of(kind, ch):
    up = ch == 0 if kind == "a" else ch % 2 == 0
    return 1 if up else -1


def arrival(kind, step, other, ch):
    if step == 0:
        return [(kind, "far", 0, 0, ch)] if other else []
    if other and kind == "b" and ch in LATE:
        return [(kind, "far", step, 0, ch)]
    if step == 2:
        return [(kind, "pass", step2_of(kind, ch), other, ch)]
    return [(kind, "ring", step, other, ch)]


def weight_keys(kind):
    return [t["key"] for t in transfers() if t["key"][0] in (kind + "p", kind + "s")]


def computes():
    todo = []

    def add(key, time, deps, rank, sends=()):
        todo.append(dict(key=key, time=time, deps=deps, rank=rank, sends=list(sends), link=None))

    spots = [(other, step) for other in (0, 1) for step in (0, 1, -1, 2)]
    for part in "sp":
        for ch in (0, 1):
            lo, hi = COLS[part][ch]
            add(("merge", part, ch), 1.2 + 4.0 * (hi - lo) / D, [], -1)
    add(("columns",), 2.0, [], -0.5)
    stats = []
    for other, step in spots:
        for twin in (0, 1):
            deps = []
            for ch in range(len(T1_CHUNKS)):
                deps += [("a", "pair", step, other, ch)] if twin else arrival("a", step, other, ch)
            add(("stat", other, step, twin), 0.6, deps + [("columns",)], 0)
            stats.append(("stat", other, step, twin))
    add(("moments",), 0.2, stats + [("columns",)], 1)
    for other, step in spots:
        for twin in (0, 1):
            sends = []
            if not twin:
                for ch in range(len(T1_CHUNKS)):
                    if (other, step) != (0, 0):
                        sends.append(("a", "pair", step, other, ch))
                    if step == 0 and other == 1:
                        sends += [("a", "ring", 1, 1, ch), ("a", "ring", -1, 1, ch)]
                    if step == step2_of("a", ch):
                        sends.append(("a", "pass", step, other, ch))
            add(("norm", other, step, twin), 0.8, [("moments",)], 2, sends)
    norms = [("norm", o, s, t) for o, s in spots for t in (0, 1)]
    for s in range(4):
        add(("qkv", s), 3.2, norms + weight_keys("v"), 3 + s)
        deps = [("qkv", s)] + ([("h", "half", 0, 0, s - 2)] if s >= 2 else [])
        add(("attend", s), 1.5 if s < 2 else 2.2, deps, 2.5)
    for other, step in spots:
        for twin in (0, 1):
            for pair in (0, 1):
                deps = weight_keys("o")
                for ch in (2 * pair, 2 * pair + 1):
                    if twin:
                        deps += [("b", "pair", step, other, ch)]
                    elif (other, step) == (0, 0):
                        deps += [("attend", ch)]
                    else:
                        deps += arrival("b", step, other, ch)
                add(("out", other, step, twin, pair), 0.6, deps, 50)
    return todo


def schedule():
    left = transfers() + computes()
    for t in left:
        rate = 200e3 if t["link"] == "core" else 45e3
        if t["link"] is not None:
            t["time"] = t["size"] / rate
    done, free, order, now = {}, {}, [], 0.0
    while left:
        best, later = None, []
        for t in left:
            if not all(d in done for d in t["deps"]):
                continue
            ready = max([0.0] + [done[d] for d in t["deps"]])
            if t["link"] is not None:
                ready = max(ready, free.get(t["link"], 0.0) - SLACK)
            if ready > now:
                later.append(ready)
                continue
            score = (t["link"] is None, t["rank"])
            if best is None or score < best[0]:
                best = (score, t)
        if best is None:
            now = min(later)
            continue
        t = best[1]
        if t["link"] is None:
            now += t["time"]
            done[t["key"]] = now
        else:
            now += 0.1
            free[t["link"]] = max(now, free.get(t["link"], 0.0)) + t["time"]
            done[t["key"]] = free[t["link"]] + 1.5
        order.append(t)
        left.remove(t)
    return order, done


def fused(
    hidden_ref, w_ref, down_ref, lengths_ref, up_ref, gain_ref, shift_ref, cos_ref, sin_ref, out_ref,
    t_ref, mask_ref, bias_ref, up_s, t1, w1, w2, t2, relay1, relay2, qkv_s, half_s, sums, moments, acc, w_f, down_f, affine, send, recv, local,
):
    row, col = lax.axis_index("row"), lax.axis_index("col")
    xh, y, core = row // 8, row // 2 % 4, row % 2
    z, xl = col // 2, col % 2

    def at(dxh=0, dy=0, dcore=0, dz=0, dxl=0):
        r = (xh + dxh) % 2 * 8 + (y + dy + 4) % 4 * 2 + (core + dcore) % 2
        c = (z + dz + 4) % 4 * 2 + (xl + dxl) % 2
        return r, c

    order, done = schedule()
    peers = [at(dy=1), at(dy=-1), at(dcore=1), at(dz=1), at(dz=-1), at(dxl=1), at(dxh=1, dxl=1)]
    barrier = pltpu.get_barrier_semaphore()
    for peer in peers:
        pl.semaphore_signal(barrier, inc=1, device_id=peer, device_id_type=MESH)
    mine = pltpu.make_async_copy(
        hidden_ref.at[:, pl.ds(pl.multiple_of(col * TOK, TOK), TOK)], t_ref, local.at[0]
    )
    mine.start()
    fetch = {}
    for i, (part, ch) in enumerate(("s0", "s1", "p0", "p1")):
        lo, hi = COLS[part][int(ch)]
        cols = pl.ds(lo, hi - lo)
        fetch[part, int(ch)] = [
            pltpu.make_async_copy(w_ref.at[:, cols], w_f.at[:, cols], local.at[2 * i + 1]),
            pltpu.make_async_copy(down_ref.at[:, cols], down_f.at[:, cols], local.at[2 * i + 2]),
        ]
    for c in sum(fetch.values(), []):
        c.start()

    def pieces(x):
        one = x.astype(jnp.bfloat16)
        rest = x - one.astype(jnp.float32)
        two = rest.astype(jnp.bfloat16)
        return one, two, (rest - two.astype(jnp.float32)).astype(jnp.bfloat16)

    def product(x, y):
        return jnp.dot(x, y, preferred_element_type=jnp.float32)

    def prepare_up():
        rank = up_ref.shape[1]
        r = lax.broadcasted_iota(jnp.int32, (rank, 4 * rank), 0)
        c = lax.broadcasted_iota(jnp.int32, (rank, 4 * rank), 1)
        spread = jnp.where(c % rank == r, 1.0, 0.0).astype(jnp.bfloat16)
        r = lax.broadcasted_iota(jnp.int32, (4 * SHARD, 4 * rank), 0)
        c = lax.broadcasted_iota(jnp.int32, (4 * SHARD, 4 * rank), 1) // rank * SHARD
        inside = (r >= c) & (r < c + SHARD)
        for i, piece in enumerate(pieces(up_ref[...] * adapter_scale)):
            wide = jnp.where(inside, product(piece, spread), 0.0)
            up_s[pl.ds(4 * SHARD * i, 4 * SHARD), :] = wide.astype(jnp.bfloat16)

    sums[...] = jnp.zeros_like(sums)
    acc[...] = jnp.zeros_like(acc)
    prepare_up()
    mine.wait()
    pl.semaphore_wait(barrier, len(peers))

    def protein(c, s):
        return (2 * (1 - c) + s) % 4

    def make(i, key):
        kind, what, step, other, ch = key

        def copy(src, dst, to):
            return pltpu.make_async_remote_copy(
                src_ref=src, dst_ref=dst, send_sem=send.at[i], recv_sem=recv.at[i],
                device_id=to, device_id_type=MESH,
            )

        if kind == "h":
            src = qkv_s.at[ch, :, pl.ds((1 - core) * 256, HALF), :]
            return copy(src, half_s.at[ch], at(dcore=1))
        if kind in ("a", "b"):
            def block(r):
                if kind == "a":
                    lo, hi = T1_CHUNKS[ch]
                    return t1.at[pl.ds(r * PART + lo, hi - lo)]
                return t2.at[r, ch, pl.ds(0, 256 if ch < 2 else 384)]

            def via():
                if kind == "a":
                    lo, hi = T1_CHUNKS[ch]
                    return relay1.at[pl.ds(lo, hi - lo)]
                if step:
                    return relay2.at[3 + step % 4, pl.ds(0, 256 if ch < 2 else 384)]
                return relay2.at[ch, pl.ds(0, 256 if ch < 2 else 384)]

            def source():
                if kind == "a":
                    lo, hi = T1_CHUNKS[ch]
                    return t_ref.at[pl.ds(lo, hi - lo)]
                return block(row)

            up = step2_of(kind, ch) == 1
            if step > 0 and what in ("hop", "far"):
                up = not up
            one, two = at(dxl=1), at(dxh=1, dxl=1)
            if not up:
                one, two = two, one
            if what == "hop":
                return copy(block(at(dy=-step)[0]) if step else source(), via(), one)
            if what == "far":
                return copy(via(), block(at(dxh=0 if up else 1, dy=-step)[0]), two)
            if what == "ring":
                slot, to = at(dxh=other), at(dy=step)
            elif what == "pass":
                slot, to = at(dxh=other, dy=-step), at(dy=step)
            else:
                slot, to = at(dxh=other, dy=-step), at(dcore=1)
            mine = other == 0 and (what == "ring" or what == "pair" and step == 0)
            return copy(source() if mine else block(slot[0]), block(slot[0]), to)
        lo, hi = COLS[kind[1]][ch]
        whole, count = (w1, W1) if kind[0] == "v" else (w2, W2)
        if what == "x":
            slot, to = at(dz=-step), at(dxl=1)
        elif what == "ring":
            slot, to = at(dxl=other), at(dz=step)
        else:
            slot, to = at(dxl=other, dz=-step), at(dz=step)
        dst = whole.at[pl.ds(slot[1] * count, count), pl.ds(lo, hi - lo)]
        return copy(dst, dst, to)

    def merge(part, ch):
        for c in fetch[part, ch]:
            c.wait()

        up = up_s[...]
        rows = 4 * SHARD
        lo, hi = COLS[part][ch]

        def body(i, carry):
            cols = pl.ds(pl.multiple_of(lo + i * 256, 256), 256)
            one, two, three = pieces(down_f[:, cols])
            a = product(up, one)
            b = product(up[: 2 * rows], two)
            total = a[2 * rows :] + b[rows:] + product(up[:rows], three)
            total = total + (a[rows : 2 * rows] + b[:rows])
            merged = (w_f[:, cols] + (total + a[:rows])).astype(jnp.bfloat16)
            w1[pl.ds(pl.multiple_of(col * W1, W1), W1), cols] = merged[:W1]
            w2[pl.ds(pl.multiple_of(col * W2, W2), W2), cols] = merged[W2_FROM:]
            return carry

        lax.fori_loop(0, (hi - lo) // 256, body, 0, unroll=True)

    def columns():
        lane = lax.broadcasted_iota(jnp.int32, lengths_ref.shape, 1)
        for p in range(4):
            length = jnp.sum(jnp.where(lane == col * 4 + p, lengths_ref[...], 0), axis=1, keepdims=True)
            across = lax.broadcasted_iota(jnp.int32, (1, LEN), 1) < length
            mask_ref[:, pl.ds(p * LEN, LEN)] = jnp.where(across, 1.0, 0.0)
            down = lax.broadcasted_iota(jnp.int32, (LEN, 1), 0) < length
            bias_ref[pl.ds(p * LEN, LEN), :] = jnp.where(down, 0.0, -jnp.inf)
        for which, ref in enumerate((gain_ref, shift_ref)):
            for j in range(D // 1024):
                turned = ref[pl.ds(8 * j, 8), :].T
                for i in range(8):
                    affine[pl.ds((8 * j + i) * 128, 128), which : which + 1] = turned[:, i : i + 1]

    def slot_of(other, step, twin):
        return at(dxh=other, dy=-step, dcore=twin)[0]

    def place():
        t1[pl.ds(pl.multiple_of(row * PART, 16), PART), :] = t_ref[...]

    def stat(other, step, twin):
        if (other, step, twin) == (0, 0, 0):
            place()
        base = slot_of(other, step, twin) * PART

        def body(i, carry):
            one, two = carry
            x = t1[pl.ds(pl.multiple_of(base + i * 16, 16), 16), :].astype(jnp.float32) * mask_ref[...]
            return one + x[:8] + x[8:], two + x[:8] * x[:8] + x[8:] * x[8:]

        one, two = lax.fori_loop(0, PART // 16, body, (sums[0], sums[1]))
        sums[0] = one
        sums[1] = two

    def get_moments():
        average = jnp.sum(sums[0], axis=0, keepdims=True) / D
        variance = jnp.sum(sums[1], axis=0, keepdims=True) / D - average * average
        moments[0] = average
        moments[1] = lax.rsqrt(variance + ln_eps)

    def norm(other, step, twin):
        base = slot_of(other, step, twin) * PART

        def body(i, carry):
            here = pl.ds(pl.multiple_of(base + i * 16, 16), 16)
            x = t1[here, :].astype(jnp.float32) * mask_ref[...]
            gain = affine[here, 0:1]
            shift = affine[here, 1:2]
            t1[here, :] = ((x - moments[0]) * moments[1] * gain + shift).astype(jnp.bfloat16)
            return carry

        lax.fori_loop(0, PART // 16, body, 0)

    def qkv(s):
        lanes = pl.ds(pl.multiple_of(protein(core, s) * LEN, LEN), LEN)
        for m in range(2):
            result = jnp.dot(
                w1[pl.ds(m * 512, 512), :], t1[:, lanes], preferred_element_type=jnp.float32
            )
            for j in range(4):
                for k in range(3):
                    qkv_s[s, k, pl.ds((m * 4 + j) * SHARD, SHARD), :] = result[
                        j * W1 + k * SHARD : j * W1 + (k + 1) * SHARD
                    ]

    def head(first, second, keys, s, rows):
        cosine, sine = cos_ref[...], sin_ref[...]

        def rotate(k):
            u, v = first[k], second[k]
            return jnp.concatenate([u * cosine - v * sine, v * cosine + u * sine], axis=0).astype(jnp.bfloat16)

        queries, key_rows = rotate(0), rotate(1)
        value_rows = jnp.concatenate([first[2], second[2]], axis=0).astype(jnp.bfloat16)
        scores = lax.dot_general(
            key_rows, queries, (((0,), (0,)), ((), ())), preferred_element_type=jnp.float32
        ) * HEAD ** (-0.5)
        scores = scores + keys
        exponent = jnp.exp(scores - jnp.max(scores, axis=0, keepdims=True))
        soft = (exponent * (1.0 / jnp.sum(exponent, axis=0, keepdims=True))).astype(jnp.bfloat16)
        got = jnp.dot(value_rows, soft, preferred_element_type=jnp.float32)
        t2[row, s, pl.ds(rows, HEAD), :] = got.astype(jnp.bfloat16)

    def attend(s):
        keys = bias_ref[pl.ds(pl.multiple_of(protein(core, s) * LEN, LEN), LEN), :]
        for h in range(2):
            start = core * HALF + h * HEAD
            first = [qkv_s[s, k, pl.ds(pl.multiple_of(start, HALF), HALF), :] for k in range(3)]
            second = [qkv_s[s, k, pl.ds(pl.multiple_of(start + HALF, HALF), HALF), :] for k in range(3)]
            head(first, second, keys, s, h * HEAD)
        if s >= 2:
            first, second = [], []
            for k in range(3):
                mine = qkv_s[s, k, pl.ds(pl.multiple_of((1 - core) * 256, HALF), HALF), :]
                came = half_s[s - 2, k]
                first.append(jnp.where(core == 0, mine, came))
                second.append(jnp.where(core == 0, came, mine))
            head(first, second, keys, s, 256)

    def project(other, step, twin, pair):
        r = slot_of(other, step, twin)
        chip, c = r // 2, r % 2
        cols = pl.ds(pl.multiple_of(chip * 640 + c * 384, 128), 256)
        middle = pl.ds(pl.multiple_of(chip * 640 + 256, 128), 128)
        for s in (2 * pair, 2 * pair + 1):
            p = protein(c, s)
            value = jnp.dot(w2[:, cols], t2[r, s, 0:256, :], preferred_element_type=jnp.float32)
            if pair:
                value += jnp.dot(w2[:, middle], t2[r, s, 256:384, :], preferred_element_type=jnp.float32)
            acc[p] += value

    copies, waited, gone = {}, set(), set()
    for i, t in enumerate(order):
        key = t["key"]
        for dep in t["deps"]:
            if dep in copies and dep not in waited:
                copies[dep].wait_recv()
                waited.add(dep)
        if t["link"] is not None:
            copies[key] = make(len(copies), key)
            copies[key].start()
            continue
        for dep in t["sends"]:
            copies[dep].wait_send()
            gone.add(dep)
        dict(merge=merge, columns=columns, stat=stat, moments=get_moments, norm=norm, qkv=qkv, attend=attend, out=project)[key[0]](*key[1:])
    for key in sorted(copies, key=lambda k: done[k]):
        if key not in waited:
            copies[key].wait_recv()
        if key not in gone:
            copies[key].wait_send()
    for j in range(4):
        for p in range(4):
            value = jnp.concatenate(
                [acc[p, pl.ds(96 * j + 8, SHARD), :], acc[p, pl.ds(96 * j + 56, SHARD), :]], axis=0
            )
            lanes = pl.ds(p * LEN, LEN)
            rest = t_ref[pl.ds(80 * j, 80), lanes].astype(jnp.float32) * mask_ref[:, lanes]
            out_ref[pl.ds(80 * j, 80), lanes] = (rest + value).astype(jnp.bfloat16)


def run_fused(*args):
    count = len(transfers())
    vmem, hbm = pl.BlockSpec(memory_space=pltpu.VMEM), pl.BlockSpec(memory_space=pl.ANY)
    return pl.pallas_call(
        fused,
        out_shape=jax.ShapeDtypeStruct((PART, TOK), jnp.bfloat16),
        in_specs=[hbm] * 3 + [vmem] * 6,
        out_specs=vmem,
        scratch_shapes=[
            pltpu.VMEM((PART, TOK), jnp.bfloat16),
            pltpu.VMEM((1, TOK), jnp.float32),
            pltpu.VMEM((TOK, 1), jnp.float32),
            pltpu.VMEM((12 * SHARD, 256), jnp.bfloat16),
            pltpu.VMEM((D, TOK), jnp.bfloat16),
            pltpu.VMEM((8 * W1, D), jnp.bfloat16),
            pltpu.VMEM((8 * W2, D), jnp.bfloat16),
            pltpu.VMEM((16, 4, 384, LEN), jnp.bfloat16),
            pltpu.VMEM((PART, TOK), jnp.bfloat16),
            pltpu.VMEM((7, 384, LEN), jnp.bfloat16),
            pltpu.VMEM((4, 3, PART, LEN), jnp.float32),
            pltpu.VMEM((2, 3, HALF, LEN), jnp.float32),
            pltpu.VMEM((2, 8, TOK), jnp.float32),
            pltpu.VMEM((2, 1, TOK), jnp.float32),
            pltpu.VMEM((4, 8 * W2, LEN), jnp.float32),
            pltpu.VMEM((4 * SHARD, D), jnp.float32),
            pltpu.VMEM((256, D), jnp.float32),
            pltpu.VMEM((D, 2), jnp.float32),
            pltpu.SemaphoreType.DMA((count,)),
            pltpu.SemaphoreType.DMA((count,)),
            pltpu.SemaphoreType.DMA((9,)),
        ],
        compiler_params=pltpu.CompilerParams(
            collective_id=0, has_side_effects=True, vmem_limit_bytes=VMEM_BYTES
        ),
    )(*args)


def rotary_tables():
    half_dim = HEAD // 2
    frequency = 10000.0 ** (-2.0 * np.arange(half_dim) / HEAD)
    angles = frequency.astype(np.float32)[:, None] * np.arange(LEN, dtype=np.float32)[None, :]
    return np.cos(angles).astype(np.float32), np.sin(angles).astype(np.float32)


def per_device(
    hidden_states,
    lengths,
    layer_norm_gain,
    layer_norm_bias,
    weights,
    adapter_down_factors,
    adapter_up_factors,
):
    rank = adapter_up_factors.shape[2]
    cosine, sine = rotary_tables()
    result = run_fused(
        hidden_states.T,
        weights.reshape(4 * SHARD, D),
        adapter_down_factors.reshape(4 * rank, D),
        lengths.reshape(1, -1),
        adapter_up_factors.reshape(4 * SHARD, rank),
        layer_norm_gain.reshape(D // 128, 128),
        layer_norm_bias.reshape(D // 128, 128),
        cosine,
        sine,
    )
    return result.T


def solution(mesh):
    in_specs = (
        P(None, "row"),
        P(),
        P(),
        P(),
        P(None, ("row", "col"), None),
        P(),
        P(None, ("row", "col"), None),
    )
    out_specs = P("col", "row")
    return jax.shard_map(
        per_device, mesh=mesh, in_specs=in_specs, out_specs=out_specs, check_vma=False
    )
```

```python
import functools

import jax
import jax.numpy as jnp
import numpy as np
from jax import lax
from jax.experimental import pallas as pl
from jax.experimental.pallas import tpu as pltpu
from jax.sharding import PartitionSpec as P

VMEM_BYTES = 60 * 1024 * 1024
MESH = pl.DeviceIdType.MESH
D = 5120
HEAD = 128
HALF = 64
LEN = 256
TOK = 1024
PART = 320
SHARD = 40
W1 = 128
W2 = 48
W2_FROM = 112

adapter_scale = 2.0
ln_eps = 1e-05

T1_CHUNKS = [(0, 160), (160, 320)]


COLS = {"p": [(0, 768), (768, 1792)], "s": [(1792, 3584), (3584, D)]}
LATE = (3,)
SLACK = 3.0
RATE = {"core": 100e3, "o": 30e3, "y": 40e3, "z": 42e3, "x": 40e3, "c": 40e3}
LATENCY = 2.5


def transfers():
    todo = []

    def add(key, link, size, deps, rank):
        todo.append(dict(key=key, link=link, size=size, deps=deps, rank=rank, time=None))

    def slots(kind, sizes, ready, rank):
        n = len(sizes)
        for ch, size in enumerate(sizes):
            up = ch < n // 2 if kind == "a" else ch % 2 == 0
            step2 = 1 if up else -1
            first, second = ("xl", "cross") if up else ("cross", "xl")
            start = ready(ch)
            late = kind == "b" and ch in LATE
            add((kind, "hop", 0, 0, ch), first, size, start, rank)
            add((kind, "far", 0, 0, ch), second, size, [(kind, "hop", 0, 0, ch)], rank)
            for other in (0, 1):
                deps = start if other == 0 else [(kind, "far", 0, 0, ch)]
                if late and other:
                    add((kind, "pair", 0, 1, ch), "core", size, deps, rank)
                    for step in (1, -1, 2):
                        first, second = second, first
                        came = (kind, "pass" if step == 2 else "ring", step2 if step == 2 else step, 0, ch)
                        add((kind, "hop", step, 0, ch), first, size, [came], rank + 1)
                        add((kind, "far", step, 0, ch), second, size, [(kind, "hop", step, 0, ch)], rank + 1)
                        add((kind, "pair", step, 1, ch), "core", size, [(kind, "far", step, 0, ch)], rank)
                    continue
                for step in (1, -1):
                    add((kind, "ring", step, other, ch), ("y", step), size, deps, rank + other)
                ring = (kind, "ring", step2, other, ch)
                add((kind, "pass", step2, other, ch), ("y", step2), size, [ring], rank + 2 + other)
                add((kind, "pair", 0, other, ch), "core", size, deps, rank)
                for step in (1, -1):
                    add((kind, "pair", step, other, ch), "core", size, [(kind, "ring", step, other, ch)], rank)
                add((kind, "pair", 2, other, ch), "core", size, [(kind, "pass", step2, other, ch)], rank)

    def rows(kind, count, rank):
        for ch in (0, 1):
            step2 = 1 if ch == 0 else -1
            p, s = kind + "p", kind + "s"
            own_p, own_s = [("merge", "p", ch)], [("merge", "s", ch)]
            size = count * (COLS["p"][ch][1] - COLS["p"][ch][0]) * 2
            for step in (1, -1):
                add((p, "ring", step, 0, ch), ("z", step), size, own_p, rank + 1)
                add((p, "x", step, 0, ch), "xl", size, [(p, "ring", step, 0, ch)], rank + 1)
            add((p, "pass", step2, 0, ch), ("z", step2), size, [(p, "ring", step2, 0, ch)], rank + 2)
            add((p, "x", 0, 0, ch), "xl", size, own_p, rank + 1)
            add((p, "x", 2, 0, ch), "xl", size, [(p, "pass", step2, 0, ch)], rank + 2)
            size = count * (COLS["s"][ch][1] - COLS["s"][ch][0]) * 2
            add((s, "x", 0, 0, ch), "xl", size, own_s, rank)
            for other in (0, 1):
                deps = own_s if other == 0 else [(s, "x", 0, 0, ch)]
                for step in (1, -1):
                    add((s, "ring", step, other, ch), ("z", step), size, deps, rank + other)
                ring = (s, "ring", step2, other, ch)
                add((s, "pass", step2, other, ch), ("z", step2), size, [ring], rank + 2 + other)

    slots("a", [(b - a) * TOK * 2 for a, b in T1_CHUNKS], lambda ch: [], 0)
    rows("v", W1, 1)
    rows("o", W2 - 16, 20)
    slots("b", [r * LEN * 2 for r in (256, 256, 384, 384)], lambda ch: [("attend", ch)], 10)
    for step in (0, 1):
        add(("h", "half", 0, 0, step), "core", 3 * HALF * LEN * 4, [("qkv", step)], -1)
    return todo


def step2_of(kind, ch):
    up = ch == 0 if kind == "a" else ch % 2 == 0
    return 1 if up else -1


def arrival(kind, step, other, ch):
    if step == 0:
        return [(kind, "far", 0, 0, ch)] if other else []
    if other and kind == "b" and ch in LATE:
        return [(kind, "far", step, 0, ch)]
    if step == 2:
        return [(kind, "pass", step2_of(kind, ch), other, ch)]
    return [(kind, "ring", step, other, ch)]


def weight_keys(kind):
    return [t["key"] for t in transfers() if t["key"][0] in (kind + "p", kind + "s")]


def computes():
    todo = []

    def add(key, time, deps, rank, sends=()):
        todo.append(dict(key=key, time=time, deps=deps, rank=rank, sends=list(sends), link=None))

    spots = [(other, step) for other in (0, 1) for step in (0, 1, -1, 2)]
    for part in "sp":
        for ch in (0, 1):
            lo, hi = COLS[part][ch]
            add(("merge", part, ch), 1.2 + 4.0 * (hi - lo) / D, [], -1)
    add(("columns",), 2.0, [], -0.5)
    stats = []
    for other, step in spots:
        for twin in (0, 1):
            deps = []
            for ch in range(len(T1_CHUNKS)):
                deps += [("a", "pair", step, other, ch)] if twin else arrival("a", step, other, ch)
            add(("stat", other, step, twin), 0.6, deps + [("columns",)], 0)
            stats.append(("stat", other, step, twin))
    add(("moments",), 0.2, stats + [("columns",)], 1)
    for other, step in spots:
        for twin in (0, 1):
            sends = []
            if not twin:
                for ch in range(len(T1_CHUNKS)):
                    if (other, step) != (0, 0):
                        sends.append(("a", "pair", step, other, ch))
                    if step == 0 and other == 1:
                        sends += [("a", "ring", 1, 1, ch), ("a", "ring", -1, 1, ch)]
                    if step == step2_of("a", ch):
                        sends.append(("a", "pass", step, other, ch))
            add(("norm", other, step, twin), 0.8, [("moments",)], 2, sends)
    norms = [("norm", o, s, t) for o, s in spots for t in (0, 1)]
    for s in range(4):
        add(("qkv", s), 3.2, norms + weight_keys("v"), 3 + s)
        deps = [("qkv", s)] + ([("h", "half", 0, 0, s - 2)] if s >= 2 else [])
        add(("attend", s), 1.5 if s < 2 else 2.2, deps, 2.5)
    add(("fill",), 0.4, weight_keys("v"), 40)
    for other, step in spots:
        for twin in (0, 1):
            for pair in (0, 1):
                deps = weight_keys("o") + [("fill",)]
                for ch in (2 * pair, 2 * pair + 1):
                    if twin:
                        deps += [("b", "pair", step, other, ch)]
                    elif (other, step) == (0, 0):
                        deps += [("attend", ch)]
                    else:
                        deps += arrival("b", step, other, ch)
                add(("out", other, step, twin, pair), 0.6, deps, 50)
    return todo


def rate_of(t):
    if t["link"] == "core" or t["link"] is None:
        return RATE["core"]
    return RATE["o"] if t["key"][0][0] == "o" else RATE[t["link"][0]]


def schedule():
    left = transfers() + computes()
    for t in left:
        rate = rate_of(t)
        if t["link"] is not None:
            t["time"] = t["size"] / rate
    done, free, order, now = {}, {}, [], 0.0
    while left:
        best, later = None, []
        for t in left:
            if not all(d in done for d in t["deps"]):
                continue
            ready = max([0.0] + [done[d] for d in t["deps"]])
            if t["link"] is not None:
                ready = max(ready, free.get(t["link"], 0.0) - SLACK)
            if ready > now:
                later.append(ready)
                continue
            score = (t["link"] is None, t["rank"])
            if best is None or score < best[0]:
                best = (score, t)
        if best is None:
            now = min(later)
            continue
        t = best[1]
        if t["link"] is None:
            now += t["time"]
            done[t["key"]] = now
        else:
            now += 0.1
            free[t["link"]] = max(now, free.get(t["link"], 0.0)) + t["time"]
            done[t["key"]] = free[t["link"]] + LATENCY
        order.append(t)
        left.remove(t)
    return order, done


def fused(
    hidden_ref, w_ref, down_ref, lengths_ref, up_ref, gain_ref, shift_ref, cos_ref, sin_ref, out_ref,
    t_ref, mask_ref, bias_ref, up_s, t1, w1, w2, t2, relay1, relay2, qkv_s, half_s, sums, moments, acc, w_f, down_f, affine, send, recv, local,
):
    row, col = lax.axis_index("row"), lax.axis_index("col")
    xh, y, core = row // 8, row // 2 % 4, row % 2
    z, xl = col // 2, col % 2

    def at(dxh=0, dy=0, dcore=0, dz=0, dxl=0):
        r = (xh + dxh) % 2 * 8 + (y + dy + 4) % 4 * 2 + (core + dcore) % 2
        c = (z + dz + 4) % 4 * 2 + (xl + dxl) % 2
        return r, c

    order, done = schedule()
    peers = [at(dy=1), at(dy=-1), at(dcore=1), at(dz=1), at(dz=-1), at(dxl=1), at(dxh=1, dxl=1)]
    barrier = pltpu.get_barrier_semaphore()
    for peer in peers:
        pl.semaphore_signal(barrier, inc=1, device_id=peer, device_id_type=MESH)
    mine = pltpu.make_async_copy(
        hidden_ref.at[:, pl.ds(pl.multiple_of(col * TOK, TOK), TOK)], t_ref, local.at[0]
    )
    mine.start()
    fetch = {}
    for i, (part, ch) in enumerate(("s0", "s1", "p0", "p1")):
        lo, hi = COLS[part][int(ch)]
        cols = pl.ds(lo, hi - lo)
        fetch[part, int(ch)] = [
            pltpu.make_async_copy(w_ref.at[:, cols], w_f.at[:, cols], local.at[2 * i + 1]),
            pltpu.make_async_copy(down_ref.at[:, cols], down_f.at[:, cols], local.at[2 * i + 2]),
        ]
    for c in sum(fetch.values(), []):
        c.start()

    def pieces(x):
        one = x.astype(jnp.bfloat16)
        rest = x - one.astype(jnp.float32)
        two = rest.astype(jnp.bfloat16)
        return one, two, (rest - two.astype(jnp.float32)).astype(jnp.bfloat16)

    def product(x, y):
        return jnp.dot(x, y, preferred_element_type=jnp.float32)

    def prepare_up():
        rank = up_ref.shape[1]
        r = lax.broadcasted_iota(jnp.int32, (rank, 4 * rank), 0)
        c = lax.broadcasted_iota(jnp.int32, (rank, 4 * rank), 1)
        spread = jnp.where(c % rank == r, 1.0, 0.0).astype(jnp.bfloat16)
        r = lax.broadcasted_iota(jnp.int32, (4 * SHARD, 4 * rank), 0)
        c = lax.broadcasted_iota(jnp.int32, (4 * SHARD, 4 * rank), 1) // rank * SHARD
        inside = (r >= c) & (r < c + SHARD)
        for i, piece in enumerate(pieces(up_ref[...] * adapter_scale)):
            wide = jnp.where(inside, product(piece, spread), 0.0)
            up_s[pl.ds(4 * SHARD * i, 4 * SHARD), :] = wide.astype(jnp.bfloat16)

    sums[...] = jnp.zeros_like(sums)
    acc[...] = jnp.zeros_like(acc)
    prepare_up()
    mine.wait()
    pl.semaphore_wait(barrier, len(peers))

    def protein(c, s):
        return (2 * (1 - c) + s) % 4

    def make(i, key):
        kind, what, step, other, ch = key

        def copy(src, dst, to):
            return pltpu.make_async_remote_copy(
                src_ref=src, dst_ref=dst, send_sem=send.at[i], recv_sem=recv.at[i],
                device_id=to, device_id_type=MESH,
            )

        if kind == "h":
            src = qkv_s.at[ch, :, pl.ds((1 - core) * 256, HALF), :]
            return copy(src, half_s.at[ch], at(dcore=1))
        if kind in ("a", "b"):
            def block(r):
                if kind == "a":
                    lo, hi = T1_CHUNKS[ch]
                    return t1.at[pl.ds(r * PART + lo, hi - lo)]
                return t2.at[r, ch, pl.ds(0, 256 if ch < 2 else 384)]

            def via():
                if kind == "a":
                    lo, hi = T1_CHUNKS[ch]
                    return relay1.at[pl.ds(lo, hi - lo)]
                if step:
                    return relay2.at[3 + step % 4, pl.ds(0, 256 if ch < 2 else 384)]
                return relay2.at[ch, pl.ds(0, 256 if ch < 2 else 384)]

            def source():
                if kind == "a":
                    lo, hi = T1_CHUNKS[ch]
                    return t_ref.at[pl.ds(lo, hi - lo)]
                return block(row)

            up = step2_of(kind, ch) == 1
            if step > 0 and what in ("hop", "far"):
                up = not up
            one, two = at(dxl=1), at(dxh=1, dxl=1)
            if not up:
                one, two = two, one
            if what == "hop":
                return copy(block(at(dy=-step)[0]) if step else source(), via(), one)
            if what == "far":
                return copy(via(), block(at(dxh=0 if up else 1, dy=-step)[0]), two)
            if what == "ring":
                slot, to = at(dxh=other), at(dy=step)
            elif what == "pass":
                slot, to = at(dxh=other, dy=-step), at(dy=step)
            else:
                slot, to = at(dxh=other, dy=-step), at(dcore=1)
            mine = other == 0 and (what == "ring" or what == "pair" and step == 0)
            return copy(source() if mine else block(slot[0]), block(slot[0]), to)
        lo, hi = COLS[kind[1]][ch]
        whole, count, skip = (w1, W1, 0) if kind[0] == "v" else (w2, W2, 16)
        if what == "x":
            slot, to = at(dz=-step), at(dxl=1)
        elif what == "ring":
            slot, to = at(dxl=other), at(dz=step)
        else:
            slot, to = at(dxl=other, dz=-step), at(dz=step)
        dst = whole.at[pl.ds(slot[1] * count + skip, count - skip), pl.ds(lo, hi - lo)]
        return copy(dst, dst, to)

    def merge(part, ch):
        for c in fetch[part, ch]:
            c.wait()

        up = up_s[...]
        rows = 4 * SHARD
        lo, hi = COLS[part][ch]

        def body(i, carry):
            cols = pl.ds(pl.multiple_of(lo + i * 256, 256), 256)
            one, two, three = pieces(down_f[:, cols])
            a = product(up, one)
            b = product(up[: 2 * rows], two)
            total = a[2 * rows :] + b[rows:] + product(up[:rows], three)
            total = total + (a[rows : 2 * rows] + b[:rows])
            merged = (w_f[:, cols] + (total + a[:rows])).astype(jnp.bfloat16)
            w1[pl.ds(pl.multiple_of(col * W1, W1), W1), cols] = merged[:W1]
            w2[pl.ds(pl.multiple_of(col * W2, W2), W2), cols] = merged[W2_FROM:]
            return carry

        lax.fori_loop(0, (hi - lo) // 256, body, 0, unroll=True)

    def columns():
        lane = lax.broadcasted_iota(jnp.int32, lengths_ref.shape, 1)
        for p in range(4):
            length = jnp.sum(jnp.where(lane == col * 4 + p, lengths_ref[...], 0), axis=1, keepdims=True)
            across = lax.broadcasted_iota(jnp.int32, (1, LEN), 1) < length
            mask_ref[:, pl.ds(p * LEN, LEN)] = jnp.where(across, 1.0, 0.0)
            down = lax.broadcasted_iota(jnp.int32, (LEN, 1), 0) < length
            bias_ref[pl.ds(p * LEN, LEN), :] = jnp.where(down, 0.0, -jnp.inf)
        for which, ref in enumerate((gain_ref, shift_ref)):
            for j in range(D // 1024):
                turned = ref[pl.ds(8 * j, 8), :].T
                for i in range(8):
                    affine[pl.ds((8 * j + i) * 128, 128), which : which + 1] = turned[:, i : i + 1]

    def slot_of(other, step, twin):
        return at(dxh=other, dy=-step, dcore=twin)[0]

    def place():
        t1[pl.ds(pl.multiple_of(row * PART, 16), PART), :] = t_ref[...]

    def stat(other, step, twin):
        if (other, step, twin) == (0, 0, 0):
            place()
        base = slot_of(other, step, twin) * PART

        def body(i, carry):
            one, two = carry
            x = t1[pl.ds(pl.multiple_of(base + i * 16, 16), 16), :].astype(jnp.float32) * mask_ref[...]
            return one + x[:8] + x[8:], two + x[:8] * x[:8] + x[8:] * x[8:]

        one, two = lax.fori_loop(0, PART // 16, body, (sums[0], sums[1]))
        sums[0] = one
        sums[1] = two

    def get_moments():
        average = jnp.sum(sums[0], axis=0, keepdims=True) / D
        variance = jnp.sum(sums[1], axis=0, keepdims=True) / D - average * average
        moments[0] = average
        moments[1] = lax.rsqrt(variance + ln_eps)

    def norm(other, step, twin):
        base = slot_of(other, step, twin) * PART

        def body(i, carry):
            here = pl.ds(pl.multiple_of(base + i * 16, 16), 16)
            x = t1[here, :].astype(jnp.float32) * mask_ref[...]
            gain = affine[here, 0:1]
            shift = affine[here, 1:2]
            t1[here, :] = ((x - moments[0]) * moments[1] * gain + shift).astype(jnp.bfloat16)
            return carry

        lax.fori_loop(0, PART // 16, body, 0)

    def qkv(s):
        lanes = pl.ds(pl.multiple_of(protein(core, s) * LEN, LEN), LEN)
        for m in range(2):
            result = jnp.dot(
                w1[pl.ds(m * 512, 512), :], t1[:, lanes], preferred_element_type=jnp.float32
            )
            for j in range(4):
                for k in range(3):
                    qkv_s[s, k, pl.ds((m * 4 + j) * SHARD, SHARD), :] = result[
                        j * W1 + k * SHARD : j * W1 + (k + 1) * SHARD
                    ]

    def fill():
        for c in range(8):
            w2[pl.ds(c * W2, 16), :] = w1[pl.ds(c * W1 + W2_FROM, 16), :]

    def head(first, second, keys, s, rows):
        cosine, sine = cos_ref[...], sin_ref[...]

        def rotate(k):
            u, v = first[k], second[k]
            return jnp.concatenate([u * cosine - v * sine, v * cosine + u * sine], axis=0).astype(jnp.bfloat16)

        queries, key_rows = rotate(0), rotate(1)
        value_rows = jnp.concatenate([first[2], second[2]], axis=0).astype(jnp.bfloat16)
        scores = lax.dot_general(
            key_rows, queries, (((0,), (0,)), ((), ())), preferred_element_type=jnp.float32
        ) * HEAD ** (-0.5)
        scores = scores + keys
        exponent = jnp.exp(scores - jnp.max(scores, axis=0, keepdims=True))
        soft = (exponent * (1.0 / jnp.sum(exponent, axis=0, keepdims=True))).astype(jnp.bfloat16)
        got = jnp.dot(value_rows, soft, preferred_element_type=jnp.float32)
        t2[row, s, pl.ds(rows, HEAD), :] = got.astype(jnp.bfloat16)

    def attend(s):
        keys = bias_ref[pl.ds(pl.multiple_of(protein(core, s) * LEN, LEN), LEN), :]
        for h in range(2):
            start = core * HALF + h * HEAD
            first = [qkv_s[s, k, pl.ds(pl.multiple_of(start, HALF), HALF), :] for k in range(3)]
            second = [qkv_s[s, k, pl.ds(pl.multiple_of(start + HALF, HALF), HALF), :] for k in range(3)]
            head(first, second, keys, s, h * HEAD)
        if s >= 2:
            first, second = [], []
            for k in range(3):
                mine = qkv_s[s, k, pl.ds(pl.multiple_of((1 - core) * 256, HALF), HALF), :]
                came = half_s[s - 2, k]
                first.append(jnp.where(core == 0, mine, came))
                second.append(jnp.where(core == 0, came, mine))
            head(first, second, keys, s, 256)

    def project(other, step, twin, pair):
        r = slot_of(other, step, twin)
        chip, c = r // 2, r % 2
        cols = pl.ds(pl.multiple_of(chip * 640 + c * 384, 128), 256)
        middle = pl.ds(pl.multiple_of(chip * 640 + 256, 128), 128)
        for s in (2 * pair, 2 * pair + 1):
            p = protein(c, s)
            value = jnp.dot(w2[:, cols], t2[r, s, 0:256, :], preferred_element_type=jnp.float32)
            if pair:
                value += jnp.dot(w2[:, middle], t2[r, s, 256:384, :], preferred_element_type=jnp.float32)
            acc[p] += value

    copies, waited, gone = {}, set(), set()
    for i, t in enumerate(order):
        key = t["key"]
        for dep in t["deps"]:
            if dep in copies and dep not in waited:
                copies[dep].wait_recv()
                waited.add(dep)
        if t["link"] is not None:
            copies[key] = make(len(copies), key)
            copies[key].start()
            continue
        for dep in t["sends"]:
            copies[dep].wait_send()
            gone.add(dep)
        dict(merge=merge, columns=columns, stat=stat, moments=get_moments, norm=norm, qkv=qkv, fill=fill, attend=attend, out=project)[key[0]](*key[1:])
    for key in sorted(copies, key=lambda k: done[k]):
        if key not in waited:
            copies[key].wait_recv()
        if key not in gone:
            copies[key].wait_send()
    for j in range(4):
        for p in range(4):
            value = jnp.concatenate(
                [acc[p, pl.ds(96 * j + 8, SHARD), :], acc[p, pl.ds(96 * j + 56, SHARD), :]], axis=0
            )
            lanes = pl.ds(p * LEN, LEN)
            rest = t_ref[pl.ds(80 * j, 80), lanes].astype(jnp.float32) * mask_ref[:, lanes]
            out_ref[pl.ds(80 * j, 80), lanes] = (rest + value).astype(jnp.bfloat16)


def run_fused(*args):
    count = len(transfers())
    vmem, hbm = pl.BlockSpec(memory_space=pltpu.VMEM), pl.BlockSpec(memory_space=pl.ANY)
    return pl.pallas_call(
        fused,
        out_shape=jax.ShapeDtypeStruct((PART, TOK), jnp.bfloat16),
        in_specs=[hbm] * 3 + [vmem] * 6,
        out_specs=vmem,
        scratch_shapes=[
            pltpu.VMEM((PART, TOK), jnp.bfloat16),
            pltpu.VMEM((1, TOK), jnp.float32),
            pltpu.VMEM((TOK, 1), jnp.float32),
            pltpu.VMEM((12 * SHARD, 256), jnp.bfloat16),
            pltpu.VMEM((D, TOK), jnp.bfloat16),
            pltpu.VMEM((8 * W1, D), jnp.bfloat16),
            pltpu.VMEM((8 * W2, D), jnp.bfloat16),
            pltpu.VMEM((16, 4, 384, LEN), jnp.bfloat16),
            pltpu.VMEM((PART, TOK), jnp.bfloat16),
            pltpu.VMEM((7, 384, LEN), jnp.bfloat16),
            pltpu.VMEM((4, 3, PART, LEN), jnp.float32),
            pltpu.VMEM((2, 3, HALF, LEN), jnp.float32),
            pltpu.VMEM((2, 8, TOK), jnp.float32),
            pltpu.VMEM((2, 1, TOK), jnp.float32),
            pltpu.VMEM((4, 8 * W2, LEN), jnp.float32),
            pltpu.VMEM((4 * SHARD, D), jnp.float32),
            pltpu.VMEM((256, D), jnp.float32),
            pltpu.VMEM((D, 2), jnp.float32),
            pltpu.SemaphoreType.DMA((count,)),
            pltpu.SemaphoreType.DMA((count,)),
            pltpu.SemaphoreType.DMA((9,)),
        ],
        compiler_params=pltpu.CompilerParams(
            collective_id=0, has_side_effects=True, vmem_limit_bytes=VMEM_BYTES
        ),
    )(*args)


def rotary_tables():
    half_dim = HEAD // 2
    frequency = 10000.0 ** (-2.0 * np.arange(half_dim) / HEAD)
    angles = frequency.astype(np.float32)[:, None] * np.arange(LEN, dtype=np.float32)[None, :]
    return np.cos(angles).astype(np.float32), np.sin(angles).astype(np.float32)


def per_device(
    hidden_states,
    lengths,
    layer_norm_gain,
    layer_norm_bias,
    weights,
    adapter_down_factors,
    adapter_up_factors,
):
    rank = adapter_up_factors.shape[2]
    cosine, sine = rotary_tables()
    result = run_fused(
        hidden_states.T,
        weights.reshape(4 * SHARD, D),
        adapter_down_factors.reshape(4 * rank, D),
        lengths.reshape(1, -1),
        adapter_up_factors.reshape(4 * SHARD, rank),
        layer_norm_gain.reshape(D // 128, 128),
        layer_norm_bias.reshape(D // 128, 128),
        cosine,
        sine,
    )
    return result.T


def solution(mesh):
    in_specs = (
        P(None, "row"),
        P(),
        P(),
        P(),
        P(None, ("row", "col"), None),
        P(),
        P(None, ("row", "col"), None),
    )
    out_specs = P("col", "row")
    return jax.shard_map(
        per_device, mesh=mesh, in_specs=in_specs, out_specs=out_specs, check_vma=False
    )
```

```python
import functools

import jax
import jax.numpy as jnp
import numpy as np
from jax import lax
from jax.experimental import pallas as pl
from jax.experimental.pallas import tpu as pltpu
from jax.sharding import PartitionSpec as P

VMEM_BYTES = 60 * 1024 * 1024
MESH = pl.DeviceIdType.MESH
D = 5120
HEAD = 128
HALF = 64
LEN = 256
TOK = 1024
PART = 320
SHARD = 40
W1 = 128
W2 = 48
W2_FROM = 112

adapter_scale = 2.0
ln_eps = 1e-05

T1_CHUNKS = [(0, 160), (160, 320)]


COLS = {"p": [(0, 768), (768, 1792)], "s": [(1792, 3584), (3584, D)]}
LATE = (3,)
SLACK = 3.0
UNROLL = 4
RATE = {"core": 100e3, "o": 30e3, "y": 40e3, "z": 42e3, "x": 40e3, "c": 40e3}
LATENCY = 2.5


def transfers():
    todo = []

    def add(key, link, size, deps, rank):
        todo.append(dict(key=key, link=link, size=size, deps=deps, rank=rank, time=None))

    def slots(kind, sizes, ready, rank):
        n = len(sizes)
        for ch, size in enumerate(sizes):
            up = ch < n // 2 if kind == "a" else ch % 2 == 0
            step2 = 1 if up else -1
            first, second = ("xl", "cross") if up else ("cross", "xl")
            start = ready(ch)
            late = kind == "b" and ch in LATE
            add((kind, "hop", 0, 0, ch), first, size, start, rank)
            add((kind, "far", 0, 0, ch), second, size, [(kind, "hop", 0, 0, ch)], rank)
            for other in (0, 1):
                deps = start if other == 0 else [(kind, "far", 0, 0, ch)]
                if late and other:
                    add((kind, "pair", 0, 1, ch), "core", size, deps, rank)
                    for step in (1, -1, 2):
                        first, second = second, first
                        came = (kind, "pass" if step == 2 else "ring", step2 if step == 2 else step, 0, ch)
                        add((kind, "hop", step, 0, ch), first, size, [came], rank + 1)
                        add((kind, "far", step, 0, ch), second, size, [(kind, "hop", step, 0, ch)], rank + 1)
                        add((kind, "pair", step, 1, ch), "core", size, [(kind, "far", step, 0, ch)], rank)
                    continue
                for step in (1, -1):
                    add((kind, "ring", step, other, ch), ("y", step), size, deps, rank + other)
                ring = (kind, "ring", step2, other, ch)
                add((kind, "pass", step2, other, ch), ("y", step2), size, [ring], rank + 2 + other)
                add((kind, "pair", 0, other, ch), "core", size, deps, rank)
                for step in (1, -1):
                    add((kind, "pair", step, other, ch), "core", size, [(kind, "ring", step, other, ch)], rank)
                add((kind, "pair", 2, other, ch), "core", size, [(kind, "pass", step2, other, ch)], rank)

    def rows(kind, count, rank):
        for ch in (0, 1):
            step2 = 1 if ch == 0 else -1
            p, s = kind + "p", kind + "s"
            own_p, own_s = [("merge", "p", ch)], [("merge", "s", ch)]
            size = count * (COLS["p"][ch][1] - COLS["p"][ch][0]) * 2
            for step in (1, -1):
                add((p, "ring", step, 0, ch), ("z", step), size, own_p, rank + 1)
                add((p, "x", step, 0, ch), "xl", size, [(p, "ring", step, 0, ch)], rank + 1)
            add((p, "pass", step2, 0, ch), ("z", step2), size, [(p, "ring", step2, 0, ch)], rank + 2)
            add((p, "x", 0, 0, ch), "xl", size, own_p, rank + 1)
            add((p, "x", 2, 0, ch), "xl", size, [(p, "pass", step2, 0, ch)], rank + 2)
            size = count * (COLS["s"][ch][1] - COLS["s"][ch][0]) * 2
            add((s, "x", 0, 0, ch), "xl", size, own_s, rank)
            for other in (0, 1):
                deps = own_s if other == 0 else [(s, "x", 0, 0, ch)]
                for step in (1, -1):
                    add((s, "ring", step, other, ch), ("z", step), size, deps, rank + other)
                ring = (s, "ring", step2, other, ch)
                add((s, "pass", step2, other, ch), ("z", step2), size, [ring], rank + 2 + other)

    slots("a", [(b - a) * TOK * 2 for a, b in T1_CHUNKS], lambda ch: [], 0)
    rows("v", W1, 1)
    rows("o", W2 - 16, 20)
    slots("b", [r * LEN * 2 for r in (256, 256, 384, 384)], lambda ch: [("attend", ch)], 10)
    for step in (0, 1):
        add(("h", "half", 0, 0, step), "core", 3 * HALF * LEN * 4, [("qkv", step)], -1)
    return todo


def step2_of(kind, ch):
    up = ch == 0 if kind == "a" else ch % 2 == 0
    return 1 if up else -1


def arrival(kind, step, other, ch):
    if step == 0:
        return [(kind, "far", 0, 0, ch)] if other else []
    if other and kind == "b" and ch in LATE:
        return [(kind, "far", step, 0, ch)]
    if step == 2:
        return [(kind, "pass", step2_of(kind, ch), other, ch)]
    return [(kind, "ring", step, other, ch)]


def weight_keys(kind):
    return [t["key"] for t in transfers() if t["key"][0] in (kind + "p", kind + "s")]


def computes():
    todo = []

    def add(key, time, deps, rank, sends=()):
        todo.append(dict(key=key, time=time, deps=deps, rank=rank, sends=list(sends), link=None))

    spots = [(other, step) for other in (0, 1) for step in (0, 1, -1, 2)]
    for part in "sp":
        for ch in (0, 1):
            lo, hi = COLS[part][ch]
            add(("merge", part, ch), 1.2 + 4.0 * (hi - lo) / D, [], -1)
    add(("columns",), 2.0, [], -0.5)
    stats = []
    for other, step in spots:
        for twin in (0, 1):
            deps = []
            for ch in range(len(T1_CHUNKS)):
                deps += [("a", "pair", step, other, ch)] if twin else arrival("a", step, other, ch)
            add(("stat", other, step, twin), 0.6, deps + [("columns",)], 0)
            stats.append(("stat", other, step, twin))
    add(("moments",), 0.2, stats + [("columns",)], 1)
    for other, step in spots:
        for twin in (0, 1):
            sends = []
            if not twin:
                for ch in range(len(T1_CHUNKS)):
                    if (other, step) != (0, 0):
                        sends.append(("a", "pair", step, other, ch))
                    if step == 0 and other == 1:
                        sends += [("a", "ring", 1, 1, ch), ("a", "ring", -1, 1, ch)]
                    if step == step2_of("a", ch):
                        sends.append(("a", "pass", step, other, ch))
            add(("norm", other, step, twin), 0.8, [("moments",)], 2, sends)
    norms = [("norm", o, s, t) for o, s in spots for t in (0, 1)]
    for s in range(4):
        add(("qkv", s), 3.2, norms + weight_keys("v"), 3 + s)
        deps = [("qkv", s)] + ([("h", "half", 0, 0, s - 2)] if s >= 2 else [])
        add(("attend", s), 1.5 if s < 2 else 2.2, deps, 2.5)
    add(("fill",), 0.4, weight_keys("v"), 40)
    for other, step in spots:
        for twin in (0, 1):
            for pair in (0, 1):
                deps = weight_keys("o") + [("fill",)]
                for ch in (2 * pair, 2 * pair + 1):
                    if twin:
                        deps += [("b", "pair", step, other, ch)]
                    elif (other, step) == (0, 0):
                        deps += [("attend", ch)]
                    else:
                        deps += arrival("b", step, other, ch)
                add(("out", other, step, twin, pair), 0.6, deps, 50)
    return todo


def rate_of(t):
    if t["link"] == "core" or t["link"] is None:
        return RATE["core"]
    return RATE["o"] if t["key"][0][0] == "o" else RATE[t["link"][0]]


def schedule():
    left = transfers() + computes()
    for t in left:
        rate = rate_of(t)
        if t["link"] is not None:
            t["time"] = t["size"] / rate
    done, free, order, now = {}, {}, [], 0.0
    while left:
        best, later = None, []
        for t in left:
            if not all(d in done for d in t["deps"]):
                continue
            ready = max([0.0] + [done[d] for d in t["deps"]])
            if t["link"] is not None:
                ready = max(ready, free.get(t["link"], 0.0) - SLACK)
            if ready > now:
                later.append(ready)
                continue
            score = (t["link"] is None, t["rank"])
            if best is None or score < best[0]:
                best = (score, t)
        if best is None:
            now = min(later)
            continue
        t = best[1]
        if t["link"] is None:
            now += t["time"]
            done[t["key"]] = now
        else:
            now += 0.1
            free[t["link"]] = max(now, free.get(t["link"], 0.0)) + t["time"]
            done[t["key"]] = free[t["link"]] + LATENCY
        order.append(t)
        left.remove(t)
    return order, done


def fused(
    hidden_ref, w_ref, down_ref, lengths_ref, up_ref, gain_ref, shift_ref, cos_ref, sin_ref, out_ref,
    t_ref, mask_ref, bias_ref, up_s, t1, w1, w2, t2, relay1, relay2, qkv_s, half_s, sums, moments, acc, w_f, down_f, affine, send, recv, local,
):
    row, col = lax.axis_index("row"), lax.axis_index("col")
    xh, y, core = row // 8, row // 2 % 4, row % 2
    z, xl = col // 2, col % 2

    def at(dxh=0, dy=0, dcore=0, dz=0, dxl=0):
        r = (xh + dxh) % 2 * 8 + (y + dy + 4) % 4 * 2 + (core + dcore) % 2
        c = (z + dz + 4) % 4 * 2 + (xl + dxl) % 2
        return r, c

    order, done = schedule()
    peers = [at(dy=1), at(dy=-1), at(dcore=1), at(dz=1), at(dz=-1), at(dxl=1), at(dxh=1, dxl=1)]
    barrier = pltpu.get_barrier_semaphore()
    for peer in peers:
        pl.semaphore_signal(barrier, inc=1, device_id=peer, device_id_type=MESH)
    mine = pltpu.make_async_copy(
        hidden_ref.at[:, pl.ds(pl.multiple_of(col * TOK, TOK), TOK)], t_ref, local.at[0]
    )
    mine.start()
    fetch = {}
    for i, (part, ch) in enumerate(("s0", "s1", "p0", "p1")):
        lo, hi = COLS[part][int(ch)]
        cols = pl.ds(lo, hi - lo)
        fetch[part, int(ch)] = [
            pltpu.make_async_copy(w_ref.at[:, cols], w_f.at[:, cols], local.at[2 * i + 1]),
            pltpu.make_async_copy(down_ref.at[:, cols], down_f.at[:, cols], local.at[2 * i + 2]),
        ]
    for c in sum(fetch.values(), []):
        c.start()

    def pieces(x):
        one = x.astype(jnp.bfloat16)
        rest = x - one.astype(jnp.float32)
        two = rest.astype(jnp.bfloat16)
        return one, two, (rest - two.astype(jnp.float32)).astype(jnp.bfloat16)

    def product(x, y):
        return jnp.dot(x, y, preferred_element_type=jnp.float32)

    def prepare_up():
        rank = up_ref.shape[1]
        r = lax.broadcasted_iota(jnp.int32, (rank, 4 * rank), 0)
        c = lax.broadcasted_iota(jnp.int32, (rank, 4 * rank), 1)
        spread = jnp.where(c % rank == r, 1.0, 0.0).astype(jnp.bfloat16)
        r = lax.broadcasted_iota(jnp.int32, (4 * SHARD, 4 * rank), 0)
        c = lax.broadcasted_iota(jnp.int32, (4 * SHARD, 4 * rank), 1) // rank * SHARD
        inside = (r >= c) & (r < c + SHARD)
        for i, piece in enumerate(pieces(up_ref[...] * adapter_scale)):
            wide = jnp.where(inside, product(piece, spread), 0.0)
            up_s[pl.ds(4 * SHARD * i, 4 * SHARD), :] = wide.astype(jnp.bfloat16)

    sums[...] = jnp.zeros_like(sums)
    acc[...] = jnp.zeros_like(acc)
    prepare_up()
    mine.wait()
    pl.semaphore_wait(barrier, len(peers))

    def protein(c, s):
        return (2 * (1 - c) + s) % 4

    def make(i, key):
        kind, what, step, other, ch = key

        def copy(src, dst, to):
            return pltpu.make_async_remote_copy(
                src_ref=src, dst_ref=dst, send_sem=send.at[i], recv_sem=recv.at[i],
                device_id=to, device_id_type=MESH,
            )

        if kind == "h":
            src = qkv_s.at[ch, :, pl.ds((1 - core) * 256, HALF), :]
            return copy(src, half_s.at[ch], at(dcore=1))
        if kind in ("a", "b"):
            def block(r):
                if kind == "a":
                    lo, hi = T1_CHUNKS[ch]
                    return t1.at[pl.ds(r * PART + lo, hi - lo)]
                return t2.at[r, ch, pl.ds(0, 256 if ch < 2 else 384)]

            def via():
                if kind == "a":
                    lo, hi = T1_CHUNKS[ch]
                    return relay1.at[pl.ds(lo, hi - lo)]
                if step:
                    return relay2.at[3 + step % 4, pl.ds(0, 256 if ch < 2 else 384)]
                return relay2.at[ch, pl.ds(0, 256 if ch < 2 else 384)]

            def source():
                if kind == "a":
                    lo, hi = T1_CHUNKS[ch]
                    return t_ref.at[pl.ds(lo, hi - lo)]
                return block(row)

            up = step2_of(kind, ch) == 1
            if step > 0 and what in ("hop", "far"):
                up = not up
            one, two = at(dxl=1), at(dxh=1, dxl=1)
            if not up:
                one, two = two, one
            if what == "hop":
                return copy(block(at(dy=-step)[0]) if step else source(), via(), one)
            if what == "far":
                return copy(via(), block(at(dxh=0 if up else 1, dy=-step)[0]), two)
            if what == "ring":
                slot, to = at(dxh=other), at(dy=step)
            elif what == "pass":
                slot, to = at(dxh=other, dy=-step), at(dy=step)
            else:
                slot, to = at(dxh=other, dy=-step), at(dcore=1)
            mine = other == 0 and (what == "ring" or what == "pair" and step == 0)
            return copy(source() if mine else block(slot[0]), block(slot[0]), to)
        lo, hi = COLS[kind[1]][ch]
        whole, count, skip = (w1, W1, 0) if kind[0] == "v" else (w2, W2, 16)
        if what == "x":
            slot, to = at(dz=-step), at(dxl=1)
        elif what == "ring":
            slot, to = at(dxl=other), at(dz=step)
        else:
            slot, to = at(dxl=other, dz=-step), at(dz=step)
        dst = whole.at[pl.ds(slot[1] * count + skip, count - skip), pl.ds(lo, hi - lo)]
        return copy(dst, dst, to)

    def merge(part, ch):
        for c in fetch[part, ch]:
            c.wait()

        up = up_s[...]
        rows = 4 * SHARD
        lo, hi = COLS[part][ch]

        def body(i, carry):
            cols = pl.ds(pl.multiple_of(lo + i * 256, 256), 256)
            one, two, three = pieces(down_f[:, cols])
            a = product(up, one)
            b = product(up[: 2 * rows], two)
            total = a[2 * rows :] + b[rows:] + product(up[:rows], three)
            total = total + (a[rows : 2 * rows] + b[:rows])
            merged = (w_f[:, cols] + (total + a[:rows])).astype(jnp.bfloat16)
            w1[pl.ds(pl.multiple_of(col * W1, W1), W1), cols] = merged[:W1]
            w2[pl.ds(pl.multiple_of(col * W2, W2), W2), cols] = merged[W2_FROM:]
            return carry

        lax.fori_loop(0, (hi - lo) // 256, body, 0, unroll=True)

    def columns():
        lane = lax.broadcasted_iota(jnp.int32, lengths_ref.shape, 1)
        for p in range(4):
            length = jnp.sum(jnp.where(lane == col * 4 + p, lengths_ref[...], 0), axis=1, keepdims=True)
            across = lax.broadcasted_iota(jnp.int32, (1, LEN), 1) < length
            mask_ref[:, pl.ds(p * LEN, LEN)] = jnp.where(across, 1.0, 0.0)
            down = lax.broadcasted_iota(jnp.int32, (LEN, 1), 0) < length
            bias_ref[pl.ds(p * LEN, LEN), :] = jnp.where(down, 0.0, -jnp.inf)
        for which, ref in enumerate((gain_ref, shift_ref)):
            for j in range(D // 1024):
                turned = ref[pl.ds(8 * j, 8), :].T
                for i in range(8):
                    affine[pl.ds((8 * j + i) * 128, 128), which : which + 1] = turned[:, i : i + 1]

    def slot_of(other, step, twin):
        return at(dxh=other, dy=-step, dcore=twin)[0]

    def place():
        t1[pl.ds(pl.multiple_of(row * PART, 16), PART), :] = t_ref[...]

    def stat(other, step, twin):
        if (other, step, twin) == (0, 0, 0):
            place()
        base = slot_of(other, step, twin) * PART

        def body(i, carry):
            one, two = carry
            x = t1[pl.ds(pl.multiple_of(base + i * 16, 16), 16), :].astype(jnp.float32) * mask_ref[...]
            return one + x[:8] + x[8:], two + x[:8] * x[:8] + x[8:] * x[8:]

        one, two = lax.fori_loop(0, PART // 16, body, (sums[0], sums[1]), unroll=UNROLL)
        sums[0] = one
        sums[1] = two

    def get_moments():
        average = jnp.sum(sums[0], axis=0, keepdims=True) / D
        variance = jnp.sum(sums[1], axis=0, keepdims=True) / D - average * average
        moments[0] = average
        moments[1] = lax.rsqrt(variance + ln_eps)

    def norm(other, step, twin):
        base = slot_of(other, step, twin) * PART

        def body(i, carry):
            here = pl.ds(pl.multiple_of(base + i * 16, 16), 16)
            x = t1[here, :].astype(jnp.float32) * mask_ref[...]
            gain = affine[here, 0:1]
            shift = affine[here, 1:2]
            t1[here, :] = ((x - moments[0]) * moments[1] * gain + shift).astype(jnp.bfloat16)
            return carry

        lax.fori_loop(0, PART // 16, body, 0, unroll=UNROLL)

    def qkv(s):
        lanes = pl.ds(pl.multiple_of(protein(core, s) * LEN, LEN), LEN)
        for m in range(2):
            result = jnp.dot(
                w1[pl.ds(m * 512, 512), :], t1[:, lanes], preferred_element_type=jnp.float32
            )
            for j in range(4):
                for k in range(3):
                    qkv_s[s, k, pl.ds((m * 4 + j) * SHARD, SHARD), :] = result[
                        j * W1 + k * SHARD : j * W1 + (k + 1) * SHARD
                    ]

    def fill():
        for c in range(8):
            w2[pl.ds(c * W2, 16), :] = w1[pl.ds(c * W1 + W2_FROM, 16), :]

    def head(first, second, keys, s, rows):
        cosine, sine = cos_ref[...], sin_ref[...]

        def rotate(k):
            u, v = first[k], second[k]
            return jnp.concatenate([u * cosine - v * sine, v * cosine + u * sine], axis=0).astype(jnp.bfloat16)

        queries, key_rows = rotate(0), rotate(1)
        value_rows = jnp.concatenate([first[2], second[2]], axis=0).astype(jnp.bfloat16)
        scores = lax.dot_general(
            key_rows, queries, (((0,), (0,)), ((), ())), preferred_element_type=jnp.float32
        ) * HEAD ** (-0.5)
        scores = scores + keys
        exponent = jnp.exp(scores - jnp.max(scores, axis=0, keepdims=True))
        soft = (exponent * (1.0 / jnp.sum(exponent, axis=0, keepdims=True))).astype(jnp.bfloat16)
        got = jnp.dot(value_rows, soft, preferred_element_type=jnp.float32)
        t2[row, s, pl.ds(rows, HEAD), :] = got.astype(jnp.bfloat16)

    def attend(s):
        keys = bias_ref[pl.ds(pl.multiple_of(protein(core, s) * LEN, LEN), LEN), :]
        for h in range(2):
            start = core * HALF + h * HEAD
            first = [qkv_s[s, k, pl.ds(pl.multiple_of(start, HALF), HALF), :] for k in range(3)]
            second = [qkv_s[s, k, pl.ds(pl.multiple_of(start + HALF, HALF), HALF), :] for k in range(3)]
            head(first, second, keys, s, h * HEAD)
        if s >= 2:
            first, second = [], []
            for k in range(3):
                mine = qkv_s[s, k, pl.ds(pl.multiple_of((1 - core) * 256, HALF), HALF), :]
                came = half_s[s - 2, k]
                first.append(jnp.where(core == 0, mine, came))
                second.append(jnp.where(core == 0, came, mine))
            head(first, second, keys, s, 256)

    def project(other, step, twin, pair):
        r = slot_of(other, step, twin)
        chip, c = r // 2, r % 2
        cols = pl.ds(pl.multiple_of(chip * 640 + c * 384, 128), 256)
        middle = pl.ds(pl.multiple_of(chip * 640 + 256, 128), 128)
        for s in (2 * pair, 2 * pair + 1):
            p = protein(c, s)
            value = jnp.dot(w2[:, cols], t2[r, s, 0:256, :], preferred_element_type=jnp.float32)
            if pair:
                value += jnp.dot(w2[:, middle], t2[r, s, 256:384, :], preferred_element_type=jnp.float32)
            acc[p] += value

    copies, waited, gone = {}, set(), set()
    for i, t in enumerate(order):
        key = t["key"]
        for dep in t["deps"]:
            if dep in copies and dep not in waited:
                copies[dep].wait_recv()
                waited.add(dep)
        if t["link"] is not None:
            copies[key] = make(len(copies), key)
            copies[key].start()
            continue
        for dep in t["sends"]:
            copies[dep].wait_send()
            gone.add(dep)
        dict(merge=merge, columns=columns, stat=stat, moments=get_moments, norm=norm, qkv=qkv, fill=fill, attend=attend, out=project)[key[0]](*key[1:])
    for key in sorted(copies, key=lambda k: done[k]):
        if key not in waited:
            copies[key].wait_recv()
        if key not in gone:
            copies[key].wait_send()
    for j in range(4):
        for p in range(4):
            value = jnp.concatenate(
                [acc[p, pl.ds(96 * j + 8, SHARD), :], acc[p, pl.ds(96 * j + 56, SHARD), :]], axis=0
            )
            lanes = pl.ds(p * LEN, LEN)
            rest = t_ref[pl.ds(80 * j, 80), lanes].astype(jnp.float32) * mask_ref[:, lanes]
            out_ref[pl.ds(80 * j, 80), lanes] = (rest + value).astype(jnp.bfloat16)


def run_fused(*args):
    count = len(transfers())
    vmem, hbm = pl.BlockSpec(memory_space=pltpu.VMEM), pl.BlockSpec(memory_space=pl.ANY)
    return pl.pallas_call(
        fused,
        out_shape=jax.ShapeDtypeStruct((PART, TOK), jnp.bfloat16),
        in_specs=[hbm] * 3 + [vmem] * 6,
        out_specs=vmem,
        scratch_shapes=[
            pltpu.VMEM((PART, TOK), jnp.bfloat16),
            pltpu.VMEM((1, TOK), jnp.float32),
            pltpu.VMEM((TOK, 1), jnp.float32),
            pltpu.VMEM((12 * SHARD, 256), jnp.bfloat16),
            pltpu.VMEM((D, TOK), jnp.bfloat16),
            pltpu.VMEM((8 * W1, D), jnp.bfloat16),
            pltpu.VMEM((8 * W2, D), jnp.bfloat16),
            pltpu.VMEM((16, 4, 384, LEN), jnp.bfloat16),
            pltpu.VMEM((PART, TOK), jnp.bfloat16),
            pltpu.VMEM((7, 384, LEN), jnp.bfloat16),
            pltpu.VMEM((4, 3, PART, LEN), jnp.float32),
            pltpu.VMEM((2, 3, HALF, LEN), jnp.float32),
            pltpu.VMEM((2, 8, TOK), jnp.float32),
            pltpu.VMEM((2, 1, TOK), jnp.float32),
            pltpu.VMEM((4, 8 * W2, LEN), jnp.float32),
            pltpu.VMEM((4 * SHARD, D), jnp.float32),
            pltpu.VMEM((256, D), jnp.float32),
            pltpu.VMEM((D, 2), jnp.float32),
            pltpu.SemaphoreType.DMA((count,)),
            pltpu.SemaphoreType.DMA((count,)),
            pltpu.SemaphoreType.DMA((9,)),
        ],
        compiler_params=pltpu.CompilerParams(
            collective_id=0, has_side_effects=True, vmem_limit_bytes=VMEM_BYTES
        ),
    )(*args)


def rotary_tables():
    half_dim = HEAD // 2
    frequency = 10000.0 ** (-2.0 * np.arange(half_dim) / HEAD)
    angles = frequency.astype(np.float32)[:, None] * np.arange(LEN, dtype=np.float32)[None, :]
    return np.cos(angles).astype(np.float32), np.sin(angles).astype(np.float32)


def per_device(
    hidden_states,
    lengths,
    layer_norm_gain,
    layer_norm_bias,
    weights,
    adapter_down_factors,
    adapter_up_factors,
):
    rank = adapter_up_factors.shape[2]
    cosine, sine = rotary_tables()
    result = run_fused(
        hidden_states.T,
        weights.reshape(4 * SHARD, D),
        adapter_down_factors.reshape(4 * rank, D),
        lengths.reshape(1, -1),
        adapter_up_factors.reshape(4 * SHARD, rank),
        layer_norm_gain.reshape(D // 128, 128),
        layer_norm_bias.reshape(D // 128, 128),
        cosine,
        sine,
    )
    return result.T


def solution(mesh):
    in_specs = (
        P(None, "row"),
        P(),
        P(),
        P(),
        P(None, ("row", "col"), None),
        P(),
        P(None, ("row", "col"), None),
    )
    out_specs = P("col", "row")
    return jax.shard_map(
        per_device, mesh=mesh, in_specs=in_specs, out_specs=out_specs, check_vma=False
    )
```

```python
import functools

import jax
import jax.numpy as jnp
import numpy as np
from jax import lax
from jax.experimental import pallas as pl
from jax.experimental.pallas import tpu as pltpu
from jax.sharding import PartitionSpec as P

VMEM_BYTES = 60 * 1024 * 1024
MESH = pl.DeviceIdType.MESH
D = 5120
HEAD = 128
HALF = 64
LEN = 256
TOK = 1024
PART = 320
SHARD = 40
W1 = 128
W2 = 48
W2_FROM = 112

adapter_scale = 2.0
ln_eps = 1e-05

T1_CHUNKS = [(0, 160), (160, 320)]


COLS = {"p": [(0, 768), (768, 1792)], "s": [(1792, 3584), (3584, D)]}
LATE = (2,)
SLACK = 3.0
UNROLL = 4
RATE = {"core": 100e3, "o": 30e3, "y": 40e3, "z": 42e3, "x": 40e3, "c": 40e3}
LATENCY = 2.5


def transfers():
    todo = []

    def add(key, link, size, deps, rank):
        todo.append(dict(key=key, link=link, size=size, deps=deps, rank=rank, time=None))

    def slots(kind, sizes, ready, rank):
        n = len(sizes)
        for ch, size in enumerate(sizes):
            up = ch < n // 2 if kind == "a" else ch % 2 == 0
            step2 = 1 if up else -1
            first, second = ("xl", "cross") if up else ("cross", "xl")
            start = ready(ch)
            late = kind == "b" and ch in LATE
            add((kind, "hop", 0, 0, ch), first, size, start, rank)
            add((kind, "far", 0, 0, ch), second, size, [(kind, "hop", 0, 0, ch)], rank)
            for other in (0, 1):
                deps = start if other == 0 else [(kind, "far", 0, 0, ch)]
                if late and other:
                    add((kind, "pair", 0, 1, ch), "core", size, deps, rank)
                    for step in (1, -1, 2):
                        first, second = second, first
                        came = (kind, "pass" if step == 2 else "ring", step2 if step == 2 else step, 0, ch)
                        add((kind, "hop", step, 0, ch), first, size, [came], rank + 1)
                        add((kind, "far", step, 0, ch), second, size, [(kind, "hop", step, 0, ch)], rank + 1)
                        add((kind, "pair", step, 1, ch), "core", size, [(kind, "far", step, 0, ch)], rank)
                    continue
                for step in (1, -1):
                    add((kind, "ring", step, other, ch), ("y", step), size, deps, rank + other)
                ring = (kind, "ring", step2, other, ch)
                add((kind, "pass", step2, other, ch), ("y", step2), size, [ring], rank + 2 + other)
                add((kind, "pair", 0, other, ch), "core", size, deps, rank)
                for step in (1, -1):
                    add((kind, "pair", step, other, ch), "core", size, [(kind, "ring", step, other, ch)], rank)
                add((kind, "pair", 2, other, ch), "core", size, [(kind, "pass", step2, other, ch)], rank)

    def rows(kind, count, rank):
        for ch in (0, 1):
            step2 = 1 if ch == 0 else -1
            p, s = kind + "p", kind + "s"
            own_p, own_s = [("merge", "p", ch)], [("merge", "s", ch)]
            size = count * (COLS["p"][ch][1] - COLS["p"][ch][0]) * 2
            for step in (1, -1):
                add((p, "ring", step, 0, ch), ("z", step), size, own_p, rank + 1)
                add((p, "x", step, 0, ch), "xl", size, [(p, "ring", step, 0, ch)], rank + 1)
            add((p, "pass", step2, 0, ch), ("z", step2), size, [(p, "ring", step2, 0, ch)], rank + 2)
            add((p, "x", 0, 0, ch), "xl", size, own_p, rank + 1)
            add((p, "x", 2, 0, ch), "xl", size, [(p, "pass", step2, 0, ch)], rank + 2)
            size = count * (COLS["s"][ch][1] - COLS["s"][ch][0]) * 2
            add((s, "x", 0, 0, ch), "xl", size, own_s, rank)
            for other in (0, 1):
                deps = own_s if other == 0 else [(s, "x", 0, 0, ch)]
                for step in (1, -1):
                    add((s, "ring", step, other, ch), ("z", step), size, deps, rank + other)
                ring = (s, "ring", step2, other, ch)
                add((s, "pass", step2, other, ch), ("z", step2), size, [ring], rank + 2 + other)

    slots("a", [(b - a) * TOK * 2 for a, b in T1_CHUNKS], lambda ch: [], 0)
    rows("v", W1, 1)
    rows("o", W2 - 16, 20)
    slots("b", [r * LEN * 2 for r in (256, 256, 384, 384)], lambda ch: [("attend", ch)], 10)
    for step in (0, 1):
        add(("h", "half", 0, 0, step), "core", 3 * HALF * LEN * 4, [("qkv", step)], -1)
    return todo


def step2_of(kind, ch):
    up = ch == 0 if kind == "a" else ch % 2 == 0
    return 1 if up else -1


def arrival(kind, step, other, ch):
    if step == 0:
        return [(kind, "far", 0, 0, ch)] if other else []
    if other and kind == "b" and ch in LATE:
        return [(kind, "far", step, 0, ch)]
    if step == 2:
        return [(kind, "pass", step2_of(kind, ch), other, ch)]
    return [(kind, "ring", step, other, ch)]


def weight_keys(kind):
    return [t["key"] for t in transfers() if t["key"][0] in (kind + "p", kind + "s")]


def computes():
    todo = []

    def add(key, time, deps, rank, sends=()):
        todo.append(dict(key=key, time=time, deps=deps, rank=rank, sends=list(sends), link=None))

    spots = [(other, step) for other in (0, 1) for step in (0, 1, -1, 2)]
    for part in "sp":
        for ch in (0, 1):
            lo, hi = COLS[part][ch]
            add(("merge", part, ch), 1.2 + 4.0 * (hi - lo) / D, [], -1)
    add(("columns",), 2.0, [], -0.5)
    stats = []
    for other, step in spots:
        for twin in (0, 1):
            deps = []
            for ch in range(len(T1_CHUNKS)):
                deps += [("a", "pair", step, other, ch)] if twin else arrival("a", step, other, ch)
            add(("stat", other, step, twin), 0.6, deps + [("columns",)], 0)
            stats.append(("stat", other, step, twin))
    add(("moments",), 0.2, stats + [("columns",)], 1)
    for other, step in spots:
        for twin in (0, 1):
            sends = []
            if not twin:
                for ch in range(len(T1_CHUNKS)):
                    if (other, step) != (0, 0):
                        sends.append(("a", "pair", step, other, ch))
                    if step == 0 and other == 1:
                        sends += [("a", "ring", 1, 1, ch), ("a", "ring", -1, 1, ch)]
                    if step == step2_of("a", ch):
                        sends.append(("a", "pass", step, other, ch))
            add(("norm", other, step, twin), 0.8, [("moments",)], 2, sends)
    norms = [("norm", o, s, t) for o, s in spots for t in (0, 1)]
    for s in range(4):
        add(("qkv", s), 3.2, norms + weight_keys("v"), 3 + s)
        deps = [("qkv", s)] + ([("h", "half", 0, 0, s - 2)] if s >= 2 else [])
        add(("attend", s), 1.5 if s < 2 else 2.2, deps, 2.5)
    add(("fill",), 0.4, weight_keys("v"), 40)
    for other, step in spots:
        for twin in (0, 1):
            for pair in (0, 1):
                deps = weight_keys("o") + [("fill",)]
                for ch in (2 * pair, 2 * pair + 1):
                    if twin:
                        deps += [("b", "pair", step, other, ch)]
                    elif (other, step) == (0, 0):
                        deps += [("attend", ch)]
                    else:
                        deps += arrival("b", step, other, ch)
                add(("out", other, step, twin, pair), 0.6, deps, 50)
    return todo


def rate_of(t):
    if t["link"] == "core" or t["link"] is None:
        return RATE["core"]
    return RATE["o"] if t["key"][0][0] == "o" else RATE[t["link"][0]]


def schedule():
    left = transfers() + computes()
    for t in left:
        rate = rate_of(t)
        if t["link"] is not None:
            t["time"] = t["size"] / rate
    done, free, order, now = {}, {}, [], 0.0
    while left:
        best, later = None, []
        for t in left:
            if not all(d in done for d in t["deps"]):
                continue
            ready = max([0.0] + [done[d] for d in t["deps"]])
            if t["link"] is not None:
                ready = max(ready, free.get(t["link"], 0.0) - SLACK)
            if ready > now:
                later.append(ready)
                continue
            score = (t["link"] is None, t["rank"])
            if best is None or score < best[0]:
                best = (score, t)
        if best is None:
            now = min(later)
            continue
        t = best[1]
        if t["link"] is None:
            now += t["time"]
            done[t["key"]] = now
        else:
            now += 0.1
            free[t["link"]] = max(now, free.get(t["link"], 0.0)) + t["time"]
            done[t["key"]] = free[t["link"]] + LATENCY
        order.append(t)
        left.remove(t)
    return order, done


def fused(
    hidden_ref, w_ref, down_ref, lengths_ref, up_ref, gain_ref, shift_ref, cos_ref, sin_ref, out_ref,
    t_ref, mask_ref, bias_ref, up_s, t1, w1, w2, t2, relay1, relay2, qkv_s, half_s, sums, moments, acc, w_f, down_f, affine, send, recv, local,
):
    row, col = lax.axis_index("row"), lax.axis_index("col")
    xh, y, core = row // 8, row // 2 % 4, row % 2
    z, xl = col // 2, col % 2

    def at(dxh=0, dy=0, dcore=0, dz=0, dxl=0):
        r = (xh + dxh) % 2 * 8 + (y + dy + 4) % 4 * 2 + (core + dcore) % 2
        c = (z + dz + 4) % 4 * 2 + (xl + dxl) % 2
        return r, c

    order, done = schedule()
    peers = [at(dy=1), at(dy=-1), at(dcore=1), at(dz=1), at(dz=-1), at(dxl=1), at(dxh=1, dxl=1)]
    barrier = pltpu.get_barrier_semaphore()
    for peer in peers:
        pl.semaphore_signal(barrier, inc=1, device_id=peer, device_id_type=MESH)
    mine = pltpu.make_async_copy(
        hidden_ref.at[:, pl.ds(pl.multiple_of(col * TOK, TOK), TOK)], t_ref, local.at[0]
    )
    mine.start()
    fetch = {}
    for i, (part, ch) in enumerate(("s0", "s1", "p0", "p1")):
        lo, hi = COLS[part][int(ch)]
        cols = pl.ds(lo, hi - lo)
        fetch[part, int(ch)] = [
            pltpu.make_async_copy(w_ref.at[:, cols], w_f.at[:, cols], local.at[2 * i + 1]),
            pltpu.make_async_copy(down_ref.at[:, cols], down_f.at[:, cols], local.at[2 * i + 2]),
        ]
    for c in sum(fetch.values(), []):
        c.start()

    def pieces(x):
        one = x.astype(jnp.bfloat16)
        rest = x - one.astype(jnp.float32)
        two = rest.astype(jnp.bfloat16)
        return one, two, (rest - two.astype(jnp.float32)).astype(jnp.bfloat16)

    def product(x, y):
        return jnp.dot(x, y, preferred_element_type=jnp.float32)

    def prepare_up():
        rank = up_ref.shape[1]
        r = lax.broadcasted_iota(jnp.int32, (rank, 4 * rank), 0)
        c = lax.broadcasted_iota(jnp.int32, (rank, 4 * rank), 1)
        spread = jnp.where(c % rank == r, 1.0, 0.0).astype(jnp.bfloat16)
        r = lax.broadcasted_iota(jnp.int32, (4 * SHARD, 4 * rank), 0)
        c = lax.broadcasted_iota(jnp.int32, (4 * SHARD, 4 * rank), 1) // rank * SHARD
        inside = (r >= c) & (r < c + SHARD)
        for i, piece in enumerate(pieces(up_ref[...] * adapter_scale)):
            wide = jnp.where(inside, product(piece, spread), 0.0)
            up_s[pl.ds(4 * SHARD * i, 4 * SHARD), :] = wide.astype(jnp.bfloat16)

    sums[...] = jnp.zeros_like(sums)
    acc[...] = jnp.zeros_like(acc)
    prepare_up()
    mine.wait()
    pl.semaphore_wait(barrier, len(peers))

    def protein(c, s):
        return (2 * (1 - c) + s) % 4

    def make(i, key):
        kind, what, step, other, ch = key

        def copy(src, dst, to):
            return pltpu.make_async_remote_copy(
                src_ref=src, dst_ref=dst, send_sem=send.at[i], recv_sem=recv.at[i],
                device_id=to, device_id_type=MESH,
            )

        if kind == "h":
            src = qkv_s.at[ch, :, pl.ds((1 - core) * 256, HALF), :]
            return copy(src, half_s.at[ch], at(dcore=1))
        if kind in ("a", "b"):
            def block(r):
                if kind == "a":
                    lo, hi = T1_CHUNKS[ch]
                    return t1.at[pl.ds(r * PART + lo, hi - lo)]
                return t2.at[r, ch, pl.ds(0, 256 if ch < 2 else 384)]

            def via():
                if kind == "a":
                    lo, hi = T1_CHUNKS[ch]
                    return relay1.at[pl.ds(lo, hi - lo)]
                if step:
                    return relay2.at[3 + step % 4, pl.ds(0, 256 if ch < 2 else 384)]
                return relay2.at[ch, pl.ds(0, 256 if ch < 2 else 384)]

            def source():
                if kind == "a":
                    lo, hi = T1_CHUNKS[ch]
                    return t_ref.at[pl.ds(lo, hi - lo)]
                return block(row)

            up = step2_of(kind, ch) == 1
            if step > 0 and what in ("hop", "far"):
                up = not up
            one, two = at(dxl=1), at(dxh=1, dxl=1)
            if not up:
                one, two = two, one
            if what == "hop":
                return copy(block(at(dy=-step)[0]) if step else source(), via(), one)
            if what == "far":
                return copy(via(), block(at(dxh=0 if up else 1, dy=-step)[0]), two)
            if what == "ring":
                slot, to = at(dxh=other), at(dy=step)
            elif what == "pass":
                slot, to = at(dxh=other, dy=-step), at(dy=step)
            else:
                slot, to = at(dxh=other, dy=-step), at(dcore=1)
            mine = other == 0 and (what == "ring" or what == "pair" and step == 0)
            return copy(source() if mine else block(slot[0]), block(slot[0]), to)
        lo, hi = COLS[kind[1]][ch]
        whole, count, skip = (w1, W1, 0) if kind[0] == "v" else (w2, W2, 16)
        if what == "x":
            slot, to = at(dz=-step), at(dxl=1)
        elif what == "ring":
            slot, to = at(dxl=other), at(dz=step)
        else:
            slot, to = at(dxl=other, dz=-step), at(dz=step)
        dst = whole.at[pl.ds(slot[1] * count + skip, count - skip), pl.ds(lo, hi - lo)]
        return copy(dst, dst, to)

    def merge(part, ch):
        for c in fetch[part, ch]:
            c.wait()

        up = up_s[...]
        rows = 4 * SHARD
        lo, hi = COLS[part][ch]

        def body(i, carry):
            cols = pl.ds(pl.multiple_of(lo + i * 256, 256), 256)
            one, two, three = pieces(down_f[:, cols])
            a = product(up, one)
            b = product(up[: 2 * rows], two)
            total = a[2 * rows :] + b[rows:] + product(up[:rows], three)
            total = total + (a[rows : 2 * rows] + b[:rows])
            merged = (w_f[:, cols] + (total + a[:rows])).astype(jnp.bfloat16)
            w1[pl.ds(pl.multiple_of(col * W1, W1), W1), cols] = merged[:W1]
            w2[pl.ds(pl.multiple_of(col * W2, W2), W2), cols] = merged[W2_FROM:]
            return carry

        lax.fori_loop(0, (hi - lo) // 256, body, 0, unroll=True)

    def columns():
        lane = lax.broadcasted_iota(jnp.int32, lengths_ref.shape, 1)
        for p in range(4):
            length = jnp.sum(jnp.where(lane == col * 4 + p, lengths_ref[...], 0), axis=1, keepdims=True)
            across = lax.broadcasted_iota(jnp.int32, (1, LEN), 1) < length
            mask_ref[:, pl.ds(p * LEN, LEN)] = jnp.where(across, 1.0, 0.0)
            down = lax.broadcasted_iota(jnp.int32, (LEN, 1), 0) < length
            bias_ref[pl.ds(p * LEN, LEN), :] = jnp.where(down, 0.0, -jnp.inf)
        for which, ref in enumerate((gain_ref, shift_ref)):
            for j in range(D // 1024):
                turned = ref[pl.ds(8 * j, 8), :].T
                for i in range(8):
                    affine[pl.ds((8 * j + i) * 128, 128), which : which + 1] = turned[:, i : i + 1]

    def slot_of(other, step, twin):
        return at(dxh=other, dy=-step, dcore=twin)[0]

    def place():
        t1[pl.ds(pl.multiple_of(row * PART, 16), PART), :] = t_ref[...]

    def stat(other, step, twin):
        if (other, step, twin) == (0, 0, 0):
            place()
        base = slot_of(other, step, twin) * PART

        def body(i, carry):
            one, two = carry
            x = t1[pl.ds(pl.multiple_of(base + i * 16, 16), 16), :].astype(jnp.float32) * mask_ref[...]
            return one + x[:8] + x[8:], two + x[:8] * x[:8] + x[8:] * x[8:]

        one, two = lax.fori_loop(0, PART // 16, body, (sums[0], sums[1]), unroll=UNROLL)
        sums[0] = one
        sums[1] = two

    def get_moments():
        average = jnp.sum(sums[0], axis=0, keepdims=True) / D
        variance = jnp.sum(sums[1], axis=0, keepdims=True) / D - average * average
        moments[0] = average
        moments[1] = lax.rsqrt(variance + ln_eps)

    def norm(other, step, twin):
        base = slot_of(other, step, twin) * PART

        def body(i, carry):
            here = pl.ds(pl.multiple_of(base + i * 16, 16), 16)
            x = t1[here, :].astype(jnp.float32) * mask_ref[...]
            gain = affine[here, 0:1]
            shift = affine[here, 1:2]
            t1[here, :] = ((x - moments[0]) * moments[1] * gain + shift).astype(jnp.bfloat16)
            return carry

        lax.fori_loop(0, PART // 16, body, 0, unroll=UNROLL)

    def qkv(s):
        lanes = pl.ds(pl.multiple_of(protein(core, s) * LEN, LEN), LEN)
        for m in range(2):
            result = jnp.dot(
                w1[pl.ds(m * 512, 512), :], t1[:, lanes], preferred_element_type=jnp.float32
            )
            for j in range(4):
                for k in range(3):
                    qkv_s[s, k, pl.ds((m * 4 + j) * SHARD, SHARD), :] = result[
                        j * W1 + k * SHARD : j * W1 + (k + 1) * SHARD
                    ]

    def fill():
        for c in range(8):
            w2[pl.ds(c * W2, 16), :] = w1[pl.ds(c * W1 + W2_FROM, 16), :]

    def head(first, second, keys, s, rows):
        cosine, sine = cos_ref[...], sin_ref[...]

        def rotate(k):
            u, v = first[k], second[k]
            return jnp.concatenate([u * cosine - v * sine, v * cosine + u * sine], axis=0).astype(jnp.bfloat16)

        queries, key_rows = rotate(0), rotate(1)
        value_rows = jnp.concatenate([first[2], second[2]], axis=0).astype(jnp.bfloat16)
        scores = lax.dot_general(
            key_rows, queries, (((0,), (0,)), ((), ())), preferred_element_type=jnp.float32
        ) * HEAD ** (-0.5)
        scores = scores + keys
        exponent = jnp.exp(scores - jnp.max(scores, axis=0, keepdims=True))
        soft = (exponent * (1.0 / jnp.sum(exponent, axis=0, keepdims=True))).astype(jnp.bfloat16)
        got = jnp.dot(value_rows, soft, preferred_element_type=jnp.float32)
        t2[row, s, pl.ds(rows, HEAD), :] = got.astype(jnp.bfloat16)

    def attend(s):
        keys = bias_ref[pl.ds(pl.multiple_of(protein(core, s) * LEN, LEN), LEN), :]
        for h in range(2):
            start = core * HALF + h * HEAD
            first = [qkv_s[s, k, pl.ds(pl.multiple_of(start, HALF), HALF), :] for k in range(3)]
            second = [qkv_s[s, k, pl.ds(pl.multiple_of(start + HALF, HALF), HALF), :] for k in range(3)]
            head(first, second, keys, s, h * HEAD)
        if s >= 2:
            first, second = [], []
            for k in range(3):
                mine = qkv_s[s, k, pl.ds(pl.multiple_of((1 - core) * 256, HALF), HALF), :]
                came = half_s[s - 2, k]
                first.append(jnp.where(core == 0, mine, came))
                second.append(jnp.where(core == 0, came, mine))
            head(first, second, keys, s, 256)

    def project(other, step, twin, pair):
        r = slot_of(other, step, twin)
        chip, c = r // 2, r % 2
        cols = pl.ds(pl.multiple_of(chip * 640 + c * 384, 128), 256)
        middle = pl.ds(pl.multiple_of(chip * 640 + 256, 128), 128)
        for s in (2 * pair, 2 * pair + 1):
            p = protein(c, s)
            value = jnp.dot(w2[:, cols], t2[r, s, 0:256, :], preferred_element_type=jnp.float32)
            if pair:
                value += jnp.dot(w2[:, middle], t2[r, s, 256:384, :], preferred_element_type=jnp.float32)
            acc[p] += value

    copies, waited, gone = {}, set(), set()
    for i, t in enumerate(order):
        key = t["key"]
        for dep in t["deps"]:
            if dep in copies and dep not in waited:
                copies[dep].wait_recv()
                waited.add(dep)
        if t["link"] is not None:
            copies[key] = make(len(copies), key)
            copies[key].start()
            continue
        for dep in t["sends"]:
            copies[dep].wait_send()
            gone.add(dep)
        dict(merge=merge, columns=columns, stat=stat, moments=get_moments, norm=norm, qkv=qkv, fill=fill, attend=attend, out=project)[key[0]](*key[1:])
    for key in sorted(copies, key=lambda k: done[k]):
        if key not in waited:
            copies[key].wait_recv()
        if key not in gone:
            copies[key].wait_send()
    for j in range(4):
        for p in range(4):
            value = jnp.concatenate(
                [acc[p, pl.ds(96 * j + 8, SHARD), :], acc[p, pl.ds(96 * j + 56, SHARD), :]], axis=0
            )
            lanes = pl.ds(p * LEN, LEN)
            rest = t_ref[pl.ds(80 * j, 80), lanes].astype(jnp.float32) * mask_ref[:, lanes]
            out_ref[pl.ds(80 * j, 80), lanes] = (rest + value).astype(jnp.bfloat16)


def run_fused(*args):
    count = len(transfers())
    vmem, hbm = pl.BlockSpec(memory_space=pltpu.VMEM), pl.BlockSpec(memory_space=pl.ANY)
    return pl.pallas_call(
        fused,
        out_shape=jax.ShapeDtypeStruct((PART, TOK), jnp.bfloat16),
        in_specs=[hbm] * 3 + [vmem] * 6,
        out_specs=vmem,
        scratch_shapes=[
            pltpu.VMEM((PART, TOK), jnp.bfloat16),
            pltpu.VMEM((1, TOK), jnp.float32),
            pltpu.VMEM((TOK, 1), jnp.float32),
            pltpu.VMEM((12 * SHARD, 256), jnp.bfloat16),
            pltpu.VMEM((D, TOK), jnp.bfloat16),
            pltpu.VMEM((8 * W1, D), jnp.bfloat16),
            pltpu.VMEM((8 * W2, D), jnp.bfloat16),
            pltpu.VMEM((16, 4, 384, LEN), jnp.bfloat16),
            pltpu.VMEM((PART, TOK), jnp.bfloat16),
            pltpu.VMEM((7, 384, LEN), jnp.bfloat16),
            pltpu.VMEM((4, 3, PART, LEN), jnp.float32),
            pltpu.VMEM((2, 3, HALF, LEN), jnp.float32),
            pltpu.VMEM((2, 8, TOK), jnp.float32),
            pltpu.VMEM((2, 1, TOK), jnp.float32),
            pltpu.VMEM((4, 8 * W2, LEN), jnp.float32),
            pltpu.VMEM((4 * SHARD, D), jnp.float32),
            pltpu.VMEM((256, D), jnp.float32),
            pltpu.VMEM((D, 2), jnp.float32),
            pltpu.SemaphoreType.DMA((count,)),
            pltpu.SemaphoreType.DMA((count,)),
            pltpu.SemaphoreType.DMA((9,)),
        ],
        compiler_params=pltpu.CompilerParams(
            collective_id=0, has_side_effects=True, vmem_limit_bytes=VMEM_BYTES
        ),
    )(*args)


def rotary_tables():
    half_dim = HEAD // 2
    frequency = 10000.0 ** (-2.0 * np.arange(half_dim) / HEAD)
    angles = frequency.astype(np.float32)[:, None] * np.arange(LEN, dtype=np.float32)[None, :]
    return np.cos(angles).astype(np.float32), np.sin(angles).astype(np.float32)


def per_device(
    hidden_states,
    lengths,
    layer_norm_gain,
    layer_norm_bias,
    weights,
    adapter_down_factors,
    adapter_up_factors,
):
    rank = adapter_up_factors.shape[2]
    cosine, sine = rotary_tables()
    result = run_fused(
        hidden_states.T,
        weights.reshape(4 * SHARD, D),
        adapter_down_factors.reshape(4 * rank, D),
        lengths.reshape(1, -1),
        adapter_up_factors.reshape(4 * SHARD, rank),
        layer_norm_gain.reshape(D // 128, 128),
        layer_norm_bias.reshape(D // 128, 128),
        cosine,
        sine,
    )
    return result.T


def solution(mesh):
    in_specs = (
        P(None, "row"),
        P(),
        P(),
        P(),
        P(None, ("row", "col"), None),
        P(),
        P(None, ("row", "col"), None),
    )
    out_specs = P("col", "row")
    return jax.shard_map(
        per_device, mesh=mesh, in_specs=in_specs, out_specs=out_specs, check_vma=False
    )
```
